256 devices in a mesh: seq: 32 (over x, z), head: 8 (over y, core).
Axes of the slice: x: 4, y: 4, z: 8, core: 2. Of those that a mesh axis runs over, the one named last changes fastest.
Arguments:
- x_in: bfloat16 [16384, 8192], P('seq', 'head'), may hold values from -1.5 to 1.5
- z_in: bfloat16 [16384, 8192], P('seq', 'head'), may hold values from -6 to 6
- bc_in: bfloat16 [16384, 8, 2, 128], P('seq', 'head'), may hold values from -3 to 3
- dt_raw: float32 [16384, 128], P('seq', 'head'), may hold values from -4 to 1000
- dt_bias: float32 [128], P('head'), may hold values from -5 to 1.5
- a_log: float32 [128], P('head'), may hold values from -8 to -2
- conv_x: bfloat16 [4, 8192], P(None, 'head'), may hold values from -3 to 3
- conv_bc: bfloat16 [4, 8, 2, 128], P(None, 'head'), may hold values from -3 to 3
- skip_gain: float32 [128], P('head'), may hold values from 0.5 to 2
- norm_gain: bfloat16 [8192], P('head'), may hold values from 0.099609375 to 1.8984375
- score_weight: bfloat16 [8192], P('head'), may hold values from -0.25 to 0.25
- passage_ids: int32 [16384], P('seq'), may hold values from 0 to 99, as said below
- teacher_logits: float32 [100], replicated, may hold values from -12 to 12
- teacher_order: int32 [100], replicated, may hold values from 0 to 99, each once
Outputs:
- mixed_out: bfloat16 [16384, 8192], P('seq', 'head')
- token_grad: float32 [16384], P('seq')
- kl_loss: float32 [], replicated
The draws below stay inside these ranges and needn't reach their ends.
Inputs may be any that keep to these rules, and one draw needn't show every extreme that they name: `passage_ids`: never falls along the tokens; each of the 100 passages has at least one token and at most 491, and one has exactly that many. Each passage appears once; teacher_logits[r] is the teacher's logit of passage teacher_order[r].
All inputs are finite; a program needn't handle non-finite values.
Results may differ from the reference program's by a relative error of at most 0.0051.
Values may be sent and summed in bfloat16 or wider, within the bound.
A program may use at most 128 MiB of HBM per device.

```python
import jax
import jax.numpy as jnp
from jax import lax

H = 128
P_SIZE = 64
N = 128
G = 8
K = 4
CH = 128
NP = 100
TOK_DEV = 512
E = 8192
TOKENS = 16384


def softplus_inverse(values):
    return values + jnp.log(-jnp.expm1(-values))


def decay_plan(key):
    base = jax.random.fold_in(key, 7)
    pick_key, fast_key, middle_key, slow_key = jax.random.split(base, 4)
    fast_share = 0.3
    slow_share = 0.2
    pick = jax.random.uniform(pick_key, (H,))
    fast = pick < fast_share
    slow = pick >= 1.0 - slow_share
    fast_span = jax.random.uniform(fast_key, (H,), minval=30.0, maxval=50.0)
    middle_span = TOK_DEV * jnp.exp(jax.random.uniform(middle_key, (H,), minval=jnp.log(0.5), maxval=jnp.log(4.0)))
    slow_span = TOKENS / jax.random.uniform(slow_key, (H,), minval=0.2, maxval=1.5)
    span = jnp.where(fast, fast_span, jnp.where(slow, slow_span, middle_span))
    step_size = 4.0 / jnp.sqrt(span)
    logarithm_coefficient = -jnp.log(span * step_size)
    shifted_bias = softplus_inverse(step_size)
    return (logarithm_coefficient, shifted_bias)


def spike_positions(key):
    return jax.random.randint(jax.random.fold_in(key, 17), (3,), 0, TOKENS)


def draw_a_log(key, part):
    logarithm_coefficient, shifted_bias = decay_plan(key)
    return logarithm_coefficient.astype(jnp.float32)


def draw_dt_bias(key, part):
    logarithm_coefficient, shifted_bias = decay_plan(key)
    return shifted_bias.astype(jnp.float32)


def draw_dt_raw(key, part):
    logarithm_coefficient, shifted_bias = decay_plan(key)
    noise_key, block_key, depth_key = jax.random.split(jax.random.fold_in(key, 13), 3)
    random_jitter = jnp.clip(0.5 * jax.random.normal(noise_key, (TOKENS, H)), -2.5, 2.5)
    offsets = jax.random.uniform(block_key, (TOKENS // TOK_DEV, H), minval=-0.7, maxval=0.7)
    random_jitter = random_jitter + jnp.repeat(offsets, TOK_DEV, axis=0)
    spike_locations = spike_positions(key)
    masked_hit = jnp.any(jnp.arange(TOKENS)[:, None] == spike_locations[None, :], axis=1)
    layer_depth = jax.random.uniform(depth_key, (TOKENS, H), minval=0.22, maxval=0.5)
    spike_amount = softplus_inverse(layer_depth * jnp.exp(-logarithm_coefficient)[None, :]) - shifted_bias[None, :]
    return jnp.where(masked_hit[:, None], spike_amount, random_jitter).astype(jnp.float32)


def draw_x_in(key, part):
    spike_locations = spike_positions(key)
    rows_index = jnp.arange(TOKENS)
    ahead = spike_locations[None, :] - rows_index[:, None]
    quiet = jnp.any((ahead >= 0) & (ahead < K), axis=1)
    values = jnp.clip(0.25 * jax.random.normal(jax.random.fold_in(key, 19), (TOKENS, E)), -1.5, 1.5)
    return jnp.where(quiet[:, None], 0.0, values).astype(jnp.bfloat16)


def draw_teacher_logits(key, part):
    values_key = jax.random.fold_in(key, 23)
    values = jnp.clip(3.0 * jax.random.normal(values_key, (NP,)), -12.0, 12.0)
    return values.astype(jnp.float32)


def draw_passage_ids(key, part):
    pick_key, weight_key = jax.random.split(jax.random.fold_in(key, 29))
    longest = 3 * TOKENS // NP
    spare = TOKENS - longest - (NP - 1)
    labels = jnp.arange(NP, dtype=jnp.int32)
    chosen = jax.random.randint(pick_key, (), 0, NP)
    shares = jax.random.randint(weight_key, (NP,), 2, 5)
    shares = jnp.where(labels == chosen, 0, shares).astype(jnp.int32)
    running = jnp.cumsum(shares).astype(jnp.int32)
    edges = spare * running // running[-1]
    extra = edges - jnp.concatenate([jnp.zeros((1,), jnp.int32), edges[:-1]])
    lengths = jnp.where(labels == chosen, longest, 1 + extra).astype(jnp.int32)
    starts = (jnp.cumsum(lengths) - lengths).astype(jnp.int32)
    positions = jnp.arange(TOKENS, dtype=jnp.int32)
    ids = jnp.sum((positions[:, None] >= starts[None, 1:]).astype(jnp.int32), axis=1)
    return ids.astype(jnp.int32)


def levels(stream_key, shape, cuts, least, high):
    loudness, own = 1.0, jax.random.fold_in(stream_key, 6)
    for dim, parts in cuts:
        draws = jnp.exp(jax.random.uniform(jax.random.fold_in(own, dim), (parts,), jnp.float32, least / len(cuts), high / len(cuts)))
        loudness = loudness * jnp.repeat(draws, shape[dim] // parts).reshape([-1 if axis == dim else 1 for axis in range(len(shape))])
    return loudness


def centred(own_key, extent, scale, bound, shards=(), kind=jnp.bfloat16):
    result = scale * jax.random.normal(own_key, extent, jnp.float32)
    if shards:
        result = result * levels(own_key, extent, shards, -0.22, 0.18)
    return jnp.clip(result, -bound, bound).astype(kind)


def setup_inputs(seed: int = 0) -> dict:
    splits = jax.random.split(jax.random.key(seed), 15)
    return {
        "x_in": draw_x_in(jax.random.fold_in(splits[14], 71), 0),
        "z_in": centred(splits[1], (TOKENS, E), 1.0, 6.0, ((0, 32), (1, 8))),
        "bc_in": centred(splits[2], (TOKENS, G, 2, N), 0.5, 3.0, ((0, 32), (1, 8))),
        "dt_raw": draw_dt_raw(jax.random.fold_in(splits[14], 71), 0),
        "dt_bias": draw_dt_bias(jax.random.fold_in(splits[14], 71), 0),
        "a_log": draw_a_log(jax.random.fold_in(splits[14], 71), 0),
        "conv_x": centred(splits[6], (K, E), K ** -0.5, 3.0, ((1, 8),)),
        "conv_bc": centred(splits[7], (K, G, 2, N), K ** -0.5, 3.0, ((1, 8),)),
        "skip_gain": jnp.clip(0.5 + 1.5 * jax.random.uniform(splits[8], (H,), jnp.float32) ** levels(splits[8], (H,), ((0, 8),), -0.2, 0.2), 0.5, 2.0),
        "norm_gain": jnp.clip(1.0 + 0.18 * jax.random.normal(splits[9], (E,), jnp.float32), 0.099609375, 1.8984375).astype(jnp.bfloat16),
        "score_weight": centred(splits[10], (E,), 512 ** -0.5, 0.25, ((0, 8),)),
        "passage_ids": draw_passage_ids(jax.random.fold_in(splits[14], 71), 0),
        "teacher_logits": draw_teacher_logits(jax.random.fold_in(splits[14], 71), 0),
        "teacher_order": jax.random.permutation(splits[13], NP).astype(jnp.int32),
    }


EPS = 1e-05
CAP = 8.0

def convolve(padded, kernel, length):
    total = jnp.zeros((length,) + padded.shape[1:], jnp.float32)
    for tap in range(kernel.shape[0]):
        total = total + padded[tap:tap + length].astype(jnp.float32) * kernel[tap].astype(jnp.float32)
    return jax.nn.silu(total).astype(jnp.bfloat16)

def block_terms(inputs, bmat, cmat, steps, rates, per_group):
    length = inputs.shape[0]
    cumul = jnp.cumsum(rates, axis=0)
    pairs = jnp.einsum('tgn,sgn->gts', cmat.astype(jnp.float32), bmat.astype(jnp.float32))
    pairs = jnp.repeat(pairs, per_group, axis=0)
    rows = lax.broadcasted_iota(jnp.int32, (length, length), 0)
    cols = lax.broadcasted_iota(jnp.int32, (length, length), 1)
    lower = (rows >= cols)[None]
    across = cumul.T
    gap = jnp.where(lower, across[:, :, None] - across[:, None, :], 0.0)
    scale_multiplier = jnp.where(lower, jnp.exp(gap), 0.0)
    weight_values = (pairs * scale_multiplier * steps.T[:, None, :]).astype(jnp.bfloat16)
    inner = jnp.einsum('hts,shp->thp', weight_values.astype(jnp.float32), inputs.astype(jnp.float32))
    tail_scale = jnp.exp(cumul[-1][None, :] - cumul) * steps
    loaded = (inputs.astype(jnp.float32) * tail_scale[:, :, None]).astype(jnp.bfloat16)
    broadcast_heads = jnp.repeat(bmat, per_group, axis=1)
    added = jnp.einsum('shn,shp->hnp', broadcast_heads.astype(jnp.float32), loaded.astype(jnp.float32))
    return (inner, added, cumul)

def reference(x_in, z_in, bc_in, dt_raw, dt_bias, a_log, conv_x, conv_bc, skip_gain, norm_gain, score_weight, passage_ids, teacher_logits, teacher_order):
    width = conv_x.shape[0]
    per_group = H // G
    x_pad = jnp.concatenate([jnp.zeros((width - 1, H * P_SIZE), jnp.bfloat16), x_in], axis=0)
    bc_pad = jnp.concatenate([jnp.zeros((width - 1, G, 2, N), jnp.bfloat16), bc_in], axis=0)
    steps_all = jax.nn.softplus(dt_raw + dt_bias[None, :])
    every_rate = -jnp.exp(a_log)[None, :] * steps_all
    gain = norm_gain.astype(jnp.float32)

    def advance(carry, index):
        start = index * CH
        x_win = lax.dynamic_slice_in_dim(x_pad, start, CH + width - 1, 0)
        bc_win = lax.dynamic_slice_in_dim(bc_pad, start, CH + width - 1, 0)
        inputs = convolve(x_win, conv_x, CH).reshape(CH, H, P_SIZE)
        bc_conv = convolve(bc_win, conv_bc, CH)
        bmat = bc_conv[:, :, 0, :]
        cmat = bc_conv[:, :, 1, :]
        steps = lax.dynamic_slice_in_dim(steps_all, start, CH, 0)
        rates = lax.dynamic_slice_in_dim(every_rate, start, CH, 0)
        inner, added, cumul = block_terms(inputs, bmat, cmat, steps, rates, per_group)
        cheads = jnp.repeat(cmat, per_group, axis=1).astype(jnp.float32)
        outer = jnp.einsum('thn,hnp->thp', cheads, carry, precision=lax.Precision.HIGHEST)
        ssd = inner + jnp.exp(cumul)[:, :, None] * outer + skip_gain[None, :, None] * inputs.astype(jnp.float32)
        gate_part = lax.dynamic_slice_in_dim(z_in, start, CH, 0)
        gated = ssd.reshape(CH, G, per_group * P_SIZE) * jax.nn.silu(gate_part.astype(jnp.float32)).reshape(CH, G, per_group * P_SIZE)
        power = lax.optimization_barrier(jnp.mean(gated * gated, axis=2, keepdims=True))
        mixed = ((gated * lax.rsqrt(power + EPS)).reshape(CH, H * P_SIZE) * gain).astype(jnp.bfloat16)
        readout = jnp.dot(mixed, score_weight, preferred_element_type=jnp.float32)
        carry = jnp.exp(cumul[-1])[:, None, None] * carry + added
        return (carry, (mixed, readout))
    start_state = jnp.zeros((H, N, P_SIZE), jnp.float32)
    closing_state, results = lax.scan(advance, start_state, jnp.arange(x_in.shape[0] // CH, dtype=jnp.int32))
    mixed_out = results[0].reshape(-1, H * P_SIZE)
    readout = results[1].reshape(-1)
    sums = jax.ops.segment_sum(readout, passage_ids, num_segments=NP)
    counts = jax.ops.segment_sum(jnp.ones(readout.shape, jnp.float32), passage_ids, num_segments=NP)
    means = sums / counts
    squash = jnp.tanh(means / CAP)
    scores = CAP * squash
    student = scores - jnp.log(jnp.sum(jnp.exp(scores)))
    teacher = jnp.zeros((NP,), jnp.float32).at[teacher_order].set(teacher_logits)
    teacher = teacher - jnp.log(jnp.sum(jnp.exp(teacher)))
    kl_loss = jnp.sum(jnp.exp(teacher) * (teacher - student))
    coef = (jnp.exp(student) - jnp.exp(teacher)) * (1.0 - squash * squash) * TOKENS / counts
    token_grad = coef[passage_ids]
    return (mixed_out, token_grad, kl_loss)
```

```python
import functools

import jax
import jax.numpy as jnp
from jax import lax
from jax.experimental import pallas as pl
from jax.experimental.pallas import tpu as pltpu
from jax.sharding import PartitionSpec as P

CH = 128
NP = 100
EPS = 1e-05
CAP = 8.0
F32 = jnp.float32
BF16 = jnp.bfloat16
MESH = pl.DeviceIdType.MESH


def nn(a, b):
    return lax.dot_general(a, b, (((1,), (0,)), ((), ())), preferred_element_type=F32)


def nt(a, b):
    return lax.dot_general(a, b, (((1,), (1,)), ((), ())), preferred_element_type=F32)


def iota(shape, dim):
    return lax.broadcasted_iota(jnp.int32, shape, dim)


def split2(v):
    high = v.astype(BF16)
    return high, (v - high.astype(F32)).astype(BF16)


def split3(v):
    high = v.astype(BF16)
    rest = v - high.astype(F32)
    mid = rest.astype(BF16)
    return high, mid, (rest - mid.astype(F32)).astype(BF16)


def column(row):
    n = row.shape[1]
    return jnp.sum(jnp.where(iota((n, n), 0) == iota((n, n), 1), row, 0.0), axis=1, keepdims=True)


def convolve(current, before, taps):
    padded = jnp.concatenate([before, current], axis=0)
    total = jnp.zeros(current.shape, F32)
    for tap in range(4):
        shifted = padded if tap == 3 else pltpu.roll(padded, 3 - tap, 0)
        total = total + shifted[16:] * taps[tap : tap + 1]
    return (total / (1.0 + jnp.exp(-total))).astype(BF16)


def kernel(
    ns,
    nh,
    x,
    z,
    bc,
    dt,
    bias,
    alog,
    convx,
    convbc,
    skip,
    gain,
    weight,
    pid,
    tlogits,
    torder,
    mixed,
    tgrad,
    kl,
    xc,
    bcc,
    bt,
    tok,
    tokb,
    carries,
    lg,
    eg,
    read,
    member,
    prow,
    tail_x,
    tail_bc,
    info,
    info_all,
    s_send,
    p1,
    e_send,
    p2,
    h_send,
    h_all,
    q_send,
    q_all,
    tail_sem,
    sems,
):
    me = lax.axis_index("seq")
    mh = lax.axis_index("head")

    def seq_peer(d):
        return lax.rem(me + d, ns)

    def head_peer(d):
        return lax.rem(mh + d, nh)

    barrier = pltpu.get_barrier_semaphore()

    @pl.loop(1, ns)
    def _(d):
        pl.semaphore_signal(barrier, inc=1, device_id={"seq": seq_peer(d)}, device_id_type=MESH)

    @pl.loop(1, nh)
    def _(d):
        pl.semaphore_signal(barrier, inc=1, device_id={"head": head_peer(d)}, device_id_type=MESH)

    steps = jax.nn.softplus(dt[...] + column(bias[...]))
    rates = -jnp.exp(column(alog[...])) * steps
    upto = (iota((CH, CH), 0) <= iota((CH, CH), 1)).astype(BF16)
    stacked = jnp.concatenate([rates[:, b * CH : (b + 1) * CH] for b in range(4)], axis=0)
    cumul = sum(nn(part, upto) for part in reversed(split3(stacked)))
    pieces = []
    for b in range(4):
        here = cumul[16 * b : 16 * b + 16]
        closing = here[:, CH - 1 :]
        f1 = split2(jnp.exp(closing - here) * steps[:, b * CH : (b + 1) * CH])
        f2 = split2(jnp.exp(here))
        rows = [f1[0].astype(F32), f1[1].astype(F32), f2[0].astype(F32), f2[1].astype(F32), here]
        pieces.append(jnp.concatenate(rows + [jnp.zeros((48, CH), F32)], axis=0))
    for b in range(4):
        turned = jnp.transpose(pieces[b])
        tok[b * CH : (b + 1) * CH] = turned
        tokb[b * CH : (b + 1) * CH] = turned.astype(BF16)
    logs = sum(tok[b * CH + CH - 1 : (b + 1) * CH] for b in range(4))

    member[...] = (iota((CH, 4 * CH), 0) == pid[...]).astype(F32).astype(BF16)
    info[0:1] = nt(jnp.ones((8, 4 * CH), BF16), member[...])[0:1]
    info[1:2] = logs
    info_all[me] = info[...]

    pl.semaphore_wait(barrier, ns - 1 + nh - 1)
    right = {"seq": seq_peer(1)}
    tails = [
        pltpu.make_async_remote_copy(
            src_ref=source.at[pl.ds(4 * CH - 16, 16)],
            dst_ref=target,
            send_sem=tail_sem.at[2 * i],
            recv_sem=tail_sem.at[2 * i + 1],
            device_id=right,
            device_id_type=MESH,
        )
        for i, (source, target) in enumerate(((x, tail_x), (bc, tail_bc)))
    ]
    for copy in tails:
        copy.start()

    def seq_copy(source, target, phase, peer):
        return pltpu.make_async_remote_copy(
            src_ref=source,
            dst_ref=target,
            send_sem=sems.at[2 * phase],
            recv_sem=sems.at[2 * phase + 1],
            device_id={"seq": peer},
            device_id_type=MESH,
        )

    def head_copy(source, target, phase, peer):
        return pltpu.make_async_remote_copy(
            src_ref=source,
            dst_ref=target,
            send_sem=sems.at[2 * phase],
            recv_sem=sems.at[2 * phase + 1],
            device_id={"head": peer},
            device_id_type=MESH,
        )

    @pl.loop(1, ns)
    def _(d):
        seq_copy(info, info_all.at[me], 0, seq_peer(d)).start()

    def conv_x(b, hp, before):
        lanes = pl.ds(pl.multiple_of(hp * CH, CH), CH)
        xc[b * CH : (b + 1) * CH, lanes] = convolve(
            x[b * CH : (b + 1) * CH, lanes].astype(F32), before, convx[:, lanes].astype(F32)
        )

    def conv_bc(b, before):
        made = convolve(bc[b * CH : (b + 1) * CH].astype(F32), before, convbc[...].astype(F32))
        bcc[b * CH : (b + 1) * CH] = made
        bt[:, b * CH : (b + 1) * CH] = jnp.transpose(made[:, :CH].astype(F32)).astype(BF16)

    for b in range(1, 4):
        conv_bc(b, bc[b * CH - 16 : b * CH].astype(F32))

    @pl.loop(0, 8)
    def _(hp):
        lanes = pl.ds(pl.multiple_of(hp * CH, CH), CH)
        for b in range(1, 4):
            conv_x(b, hp, x[b * CH - 16 : b * CH, lanes].astype(F32))

    for copy in tails:
        copy.wait()
    conv_bc(0, jnp.where(me > 0, tail_bc[...].astype(F32), 0.0))

    @pl.loop(0, 8)
    def _(hp):
        lanes = pl.ds(pl.multiple_of(hp * CH, CH), CH)
        conv_x(0, hp, jnp.where(me > 0, tail_x[:, lanes].astype(F32), 0.0))
        head_of = 2 * hp + iota((CH, CH), 1) // 64
        row = iota((CH, CH), 0)
        spread1 = ((row < 32) & (row % 16 == head_of)).astype(F32).astype(BF16)
        spread2 = ((row >= 32) & (row < 64) & (row % 16 == head_of)).astype(F32).astype(BF16)
        state = None
        ahead = jnp.ones((1, CH), F32)
        for b in range(4):
            at = slice(b * CH, (b + 1) * CH)
            factor = nn(tokb[at], spread1)
            decay = nn(tokb[at], spread2)
            loaded = (xc[at, lanes].astype(F32) * factor).astype(BF16)
            added = nn(bt[:, at], loaded)
            lg[at, lanes] = decay
            eg[at, lanes] = decay * ahead
            ahead = ahead * decay[CH - 1 :]
            if b:
                carries[b - 1, 0, :, lanes], carries[b - 1, 1, :, lanes] = split2(state)
            state = added if state is None else decay[CH - 1 :] * state + added
        state = state.astype(BF16)
        for a in range(4):
            s_send[hp * 4 + a] = state[32 * a : 32 * a + 32]

    @pl.loop(1, ns)
    def _(d):
        peer = seq_peer(d)
        seq_copy(s_send.at[peer], p1.at[me], 1, peer).start()

    p1[me] = s_send[me]

    def wait_all(phase, count, source, target):
        copy = seq_copy(source.at[pl.ds(0, count)], target.at[pl.ds(0, count)], phase, seq_peer(1))
        copy.wait_recv()

    def wait_sent(phase, count, source):
        copy = seq_copy(source.at[pl.ds(0, count)], source.at[pl.ds(0, count)], phase, seq_peer(1))
        copy.wait_send()

    def inside(hp):
        lanes = pl.ds(pl.multiple_of(hp * CH, CH), CH)
        lane = iota((CH, CH), 1)
        lower = iota((CH, CH), 0) >= lane
        first = lane < 64
        skips = jnp.sum(
            jnp.where(iota((1, CH), 1) // 64 + 2 * hp == iota((16, 1), 0), column(skip[...]), 0.0),
            axis=0,
            keepdims=True,
        )
        for b in range(4):
            at = slice(b * CH, (b + 1) * CH)
            pairs = jnp.where(lower, nn(bcc[at, CH:], bt[:, at]), 0.0)
            values = xc[at, lanes]
            halves = []
            for i in range(2):
                pick = iota((CH, CH), 1) == 64 + 2 * hp + i
                later = jnp.sum(jnp.where(pick, tok[at], 0.0), axis=1, keepdims=True)
                earlier = prow[0, 2 * hp + i, :, at]
                step = prow[1, 2 * hp + i, :, at]
                halves.append((pairs * jnp.exp(jnp.minimum(later - earlier, 0.0)) * step).astype(BF16))
            blocks = jnp.concatenate(
                [jnp.where(first, values, jnp.zeros_like(values)), jnp.where(first, jnp.zeros_like(values), values)],
                axis=0,
            )
            total = nn(jnp.concatenate(halves, axis=1), blocks) + skips * values.astype(F32)
            if b:
                outer = nn(bcc[at, CH:], carries[b - 1, 0, :, lanes]) + nn(bcc[at, CH:], carries[b - 1, 1, :, lanes])
                total = total + lg[at, lanes] * outer
            gate = z[at, lanes].astype(F32)
            gate = gate * (0.5 * jnp.tanh(0.5 * gate) + 0.5)
            lg[at, lanes] = total * gate
            eg[at, lanes] = eg[at, lanes] * gate

    for h in range(16):
        for b in range(4):
            prow[0, h, :, b * CH : (b + 1) * CH] = cumul[16 * b + h : 16 * b + h + 1]
        prow[1, h] = steps[h : h + 1]

    @pl.loop(0, 4)
    def _(hp):
        inside(hp)

    wait_all(0, ns - 1, info_all, info_all)
    lane = iota((1, CH), 1)
    kept = (lane >= 64) & (lane < 80)
    decays = jnp.where(kept, jnp.exp(jnp.where(kept, info_all[:, 1, :], 0.0)), 0.0)
    spread = (iota((CH, CH), 0) == 64 + 2 * (me // 4) + iota((CH, CH), 1) // 64).astype(F32).astype(BF16)
    decays = sum(nn(part, spread) for part in reversed(split3(decays)))
    counts = jnp.sum(info_all[:, 0, :], axis=0, keepdims=True)
    wait_all(1, ns - 1, p1, p1)
    entering = jnp.zeros((32, CH), F32)
    for j in range(ns):
        e_send[j] = entering.astype(BF16)
        if j < ns - 1:
            entering = decays[j : j + 1] * entering + p1[j].astype(F32)

    @pl.loop(1, ns)
    def _(d):
        peer = seq_peer(d)
        seq_copy(e_send.at[peer], p2.at[me], 2, peer).start()

    p2[me] = e_send[me]

    @pl.loop(4, 8)
    def _(hp):
        inside(hp)

    valid = lane < NP
    ranks = jnp.where(iota((NP, NP), 0) == torder[...], tlogits[...], 0.0)
    ranks = jnp.sum(ranks, axis=1, keepdims=True)
    teacher = jnp.sum(jnp.where(iota((NP, CH), 0) == iota((NP, CH), 1), ranks, 0.0), axis=0, keepdims=True)
    teacher = teacher - jnp.log(jnp.sum(jnp.where(valid, jnp.exp(teacher), 0.0), axis=1, keepdims=True))
    share = jnp.where(valid, jnp.exp(teacher), 0.0)
    weights = jnp.broadcast_to(weight[...].astype(F32), (16, 8 * CH)).astype(BF16)
    gains = gain[...].astype(F32)

    wait_all(2, ns - 1, p2, p2)

    @pl.loop(0, 4)
    def _(b):
        at = pl.ds(pl.multiple_of(b * CH, CH), CH)
        cmat = bcc[at, CH:]
        squares = jnp.zeros((CH, CH), F32)
        for hp in range(8):
            lanes = slice(hp * CH, (hp + 1) * CH)
            state = p2[4 * hp : 4 * hp + 4].reshape(CH, CH)
            gated = lg[at, lanes] + eg[at, lanes] * nn(cmat, state)
            lg[at, lanes] = gated
            squares = squares + gated * gated
        scale = lax.rsqrt(jnp.sum(squares, axis=1, keepdims=True) / (8 * CH) + EPS)
        for hp in range(8):
            lanes = slice(hp * CH, (hp + 1) * CH)
            mixed[at, lanes] = (lg[at, lanes] * scale * gains[:, lanes]).astype(BF16)
        read[b] = nt(weights, mixed[at, :])[0:8]

    readout = jnp.concatenate([read[b] for b in range(4)], axis=1)
    part = sum(nt(part, member[...]) for part in reversed(split3(readout)))
    h_send[...] = part[0:1]
    h_all[mh] = part[0:1]

    @pl.loop(1, nh)
    def _(d):
        head_copy(h_send, h_all.at[mh], 3, head_peer(d)).start()

    wait_all(3, nh - 1, h_all, h_all)
    total = jnp.sum(h_all[...], axis=0)
    q_send[...] = total
    q_all[me] = total

    @pl.loop(1, ns)
    def _(d):
        seq_copy(q_send, q_all.at[me], 4, seq_peer(d)).start()

    wait_all(4, ns - 1, q_all, q_all)
    sums = jnp.sum(q_all[...], axis=0)
    counts = jnp.where(valid, counts, 1.0)
    squash = jnp.tanh(sums / counts / CAP)
    scores = CAP * squash
    student = scores - jnp.log(jnp.sum(jnp.where(valid, jnp.exp(scores), 0.0), axis=1, keepdims=True))
    kl[...] = jnp.sum(share * (teacher - student), axis=1, keepdims=True)
    coef = (jnp.exp(student) - share) * (1.0 - squash * squash) * (4.0 * CH * ns) / counts
    coef = jnp.broadcast_to(jnp.where(valid, coef, 0.0), (8, CH))
    tgrad[...] = sum(nn(part, member[...]) for part in reversed(split3(coef)))[0:1]

    wait_sent(0, ns - 1, info_all)
    wait_sent(1, ns - 1, s_send)
    wait_sent(2, ns - 1, e_send)
    wait_sent(3, nh - 1, h_all)
    wait_sent(4, ns - 1, q_all)


def solution(mesh):
    ns, nh = mesh.shape["seq"], mesh.shape["head"]

    def per_device(
        x_in, z_in, bc_in, dt_raw, dt_bias, a_log, conv_x, conv_bc, skip_gain, norm_gain, score_weight, passage_ids,
        teacher_logits, teacher_order,
    ):
        vmem = pl.BlockSpec(memory_space=pltpu.VMEM)
        tokens, width = x_in.shape
        mixed, tgrad, kl = pl.pallas_call(
            functools.partial(kernel, ns, nh),
            out_shape=(
                jax.ShapeDtypeStruct((tokens, width), BF16),
                jax.ShapeDtypeStruct((1, tokens), F32),
                jax.ShapeDtypeStruct((1, 1), F32),
            ),
            in_specs=[vmem] * 14,
            out_specs=(vmem, vmem, vmem),
            scratch_shapes=[
                pltpu.VMEM((tokens, width), BF16),
                pltpu.VMEM((tokens, 2 * CH), BF16),
                pltpu.VMEM((CH, tokens), BF16),
                pltpu.VMEM((tokens, CH), F32),
                pltpu.VMEM((tokens, CH), BF16),
                pltpu.VMEM((3, 2, CH, width), BF16),
                pltpu.VMEM((tokens, width), F32),
                pltpu.VMEM((tokens, width), F32),
                pltpu.VMEM((4, 8, CH), F32),
                pltpu.VMEM((CH, tokens), BF16),
                pltpu.VMEM((2, 16, 1, tokens), F32),
                pltpu.VMEM((16, width), BF16),
                pltpu.VMEM((16, 2 * CH), BF16),
                pltpu.VMEM((2, CH), F32),
                pltpu.VMEM((ns, 2, CH), F32),
                pltpu.VMEM((ns, 32, CH), BF16),
                pltpu.VMEM((ns, 32, CH), BF16),
                pltpu.VMEM((ns, 32, CH), BF16),
                pltpu.VMEM((ns, 32, CH), BF16),
                pltpu.VMEM((1, CH), F32),
                pltpu.VMEM((nh, 1, CH), F32),
                pltpu.VMEM((1, CH), F32),
                pltpu.VMEM((ns, 1, CH), F32),
                pltpu.SemaphoreType.DMA((4,)),
                pltpu.SemaphoreType.DMA((10,)),
            ],
            compiler_params=pltpu.CompilerParams(
                collective_id=0, has_side_effects=True, vmem_limit_bytes=48 * 2**20
            ),
        )(
            x_in,
            z_in,
            bc_in.reshape(tokens, 2 * CH),
            dt_raw.T,
            dt_bias[None],
            a_log[None],
            conv_x,
            conv_bc.reshape(4, 2 * CH),
            skip_gain[None],
            norm_gain[None],
            score_weight[None],
            passage_ids[None],
            teacher_logits[None],
            teacher_order[None],
        )
        return mixed, tgrad.reshape(tokens), kl.reshape(())

    return jax.shard_map(
        per_device,
        mesh=mesh,
        in_specs=(
            P("seq", "head"), P("seq", "head"), P("seq", "head", None, None), P("seq", "head"), P("head"), P("head"),
            P(None, "head"), P(None, "head", None, None), P("head"), P("head"), P("head"), P("seq"), P(), P(),
        ),
        out_specs=(P("seq", "head"), P("seq"), P()),
        check_vma=False,
    )
```

```python
import functools

import jax
import jax.numpy as jnp
from jax import lax
from jax.experimental import pallas as pl
from jax.experimental.pallas import tpu as pltpu
from jax.sharding import PartitionSpec as P

CH = 128
NP = 100
EPS = 1e-05
CAP = 8.0
F32 = jnp.float32
BF16 = jnp.bfloat16
MESH = pl.DeviceIdType.MESH


def nn(a, b):
    return lax.dot_general(a, b, (((1,), (0,)), ((), ())), preferred_element_type=F32)


def nt(a, b):
    return lax.dot_general(a, b, (((1,), (1,)), ((), ())), preferred_element_type=F32)


def iota(shape, dim):
    return lax.broadcasted_iota(jnp.int32, shape, dim)


def split2(v):
    high = v.astype(BF16)
    return high, (v - high.astype(F32)).astype(BF16)


def split3(v):
    high = v.astype(BF16)
    rest = v - high.astype(F32)
    mid = rest.astype(BF16)
    return high, mid, (rest - mid.astype(F32)).astype(BF16)


def column(row):
    n = row.shape[1]
    return jnp.sum(jnp.where(iota((n, n), 0) == iota((n, n), 1), row, 0.0), axis=1, keepdims=True)


def silu(v):
    below = 1.0 + jnp.exp(-v)
    guess = pl.reciprocal(below, approx=True)
    return v * (guess * (2.0 - below * guess))


def convolve(current, before, taps):
    padded = jnp.concatenate([before, current], axis=0)
    total = jnp.zeros(current.shape, F32)
    for tap in range(4):
        shifted = padded if tap == 3 else pltpu.roll(padded, 3 - tap, 0)
        total = total + shifted[16:] * taps[tap : tap + 1]
    return silu(total).astype(BF16)


def spread_codes(shape, sections):
    row, lane = iota(shape, 0), iota(shape, 1)
    code = jnp.full(shape, -1, jnp.int32)
    for first, last, start, width, size in sections:
        inside = (row >= first) & (row < last) & (lane >= start) & (lane < start + width)
        code = jnp.where(inside, (row & 15) - (lane - start) // size, code)
    return code


def kernel(ns, nh, *refs):
    given, (result, tgrad, kl), held = refs[:14], refs[14:17], refs[17:31]
    x, z, bc, dt, bias, alog, convx, convbc, skip, gain, weight, pid, tlogits, torder = held
    (
        xc, cm, bt, mix, paired, tokb, tokc, spreads, codes, local, lg, eg, squares, read, member, prow, tail_x, tail_bc,
        info, info_all, s_send, p1, e_send, p2, h_send, h_all, q_send, q_all, mixed,
        in_sem, out_sem, tail_sem, sems, p2_sem,
    ) = refs[31:]
    me = lax.axis_index("seq")
    mh = lax.axis_index("head")

    def far(i):
        return 4 + (2 * lax.rem(i, 2) - 1) * ((i + 1) // 2)

    def seq_pair(i):
        return lax.rem(me // 4 + far(i), 8)

    def each_seq_peer(act):
        @pl.loop(0, ns)
        def _(t):
            peer = 4 * seq_pair(t // 4) + lax.rem(t, 4)

            @pl.when(peer != me)
            def _():
                act(peer)

    def each_head_peer(act):
        @pl.loop(0, nh - 1)
        def _(t):
            act(lax.rem(mh + far(t), nh))

    barrier = pltpu.get_barrier_semaphore()
    each_seq_peer(lambda peer: pl.semaphore_signal(barrier, inc=1, device_id={"seq": peer}, device_id_type=MESH))
    each_head_peer(lambda peer: pl.semaphore_signal(barrier, inc=1, device_id={"head": peer}, device_id_type=MESH))

    loads = [
        pltpu.make_async_copy(source, target, in_sem.at[i])
        for i, (source, target) in enumerate(zip(given, held))
    ]
    for i in (3, 4, 5, 2, 7, 0, 6, 11, 1, 8, 9, 10, 12, 13):
        loads[i].start()

    codes[...] = spread_codes((CH, 4 * CH), ((0, 32, 0, CH, 64), (32, 64, CH, CH, 64), (64, 112, 2 * CH, 2 * CH, CH)))
    for hp in range(8):
        code = spread_codes((CH, CH), ((0, 32, 0, CH, 64),))
        spreads[:, hp * CH : (hp + 1) * CH] = (code == 2 * hp).astype(F32).astype(BF16)
    squares[...] = jnp.zeros(squares.shape, F32)

    for i in (3, 4, 5):
        loads[i].wait()
    steps = jax.nn.softplus(dt[...] + column(bias[...]))
    rates = -jnp.exp(column(alog[...])) * steps
    upto = (iota((CH, CH), 0) <= iota((CH, CH), 1)).astype(F32).astype(BF16)
    stacked = jnp.concatenate([rates[:, b * CH : (b + 1) * CH] for b in range(4)], axis=0)
    cumul = sum(nn(part, upto) for part in reversed(split3(stacked)))
    logs = jnp.zeros((16, 1), F32)
    for b in reversed(range(4)):
        here = cumul[16 * b : 16 * b + 16]
        logs = logs + here[:, CH - 1 :]
        parts = split2(jnp.exp(logs - here) * steps[:, b * CH : (b + 1) * CH])
        rows = [part.astype(F32) for part in parts] + [jnp.zeros((96, CH), F32)]
        tokb[b * CH : (b + 1) * CH] = jnp.transpose(jnp.concatenate(rows, axis=0)).astype(BF16)

    even = iota((8, CH), 0) % 2 == 0
    for i in (2, 7):
        loads[i].wait()
    taps = convbc[...].astype(F32)

    def conv_bc(first, count, before):
        current = bc[2 * first : 2 * (first + count)].astype(F32)
        padded = jnp.concatenate([before, current], axis=0)
        total = jnp.zeros((count // 4, 8, CH), F32)
        for tap in range(4):
            shifted = padded if tap == 3 else pltpu.roll(padded, 2 * (3 - tap), 0)
            factor = jnp.where(even, taps[2 * tap : 2 * tap + 1], taps[2 * tap + 1 : 2 * tap + 2])
            total = total + shifted[16:].reshape(count // 4, 8, CH) * factor[None]
        mix[2 * first : 2 * (first + count)] = silu(total).reshape(2 * count, CH)

    def turn_b(b):
        bt[:, b * CH : (b + 1) * CH] = jnp.transpose(mix[pl.ds(2 * b * CH, CH, stride=2)]).astype(BF16)

    for b in range(4):
        conv_bc(b * CH, CH, bc[2 * b * CH - 16 : 2 * b * CH].astype(F32) if b else jnp.zeros((16, CH), F32))
        turn_b(b)
    for i in (0, 6):
        loads[i].wait()

    def local_state(hp):
        lanes = pl.ds(pl.multiple_of(hp * CH, CH), CH)
        factors = convx[:, lanes].astype(F32)
        loaded = []
        for b in range(4):
            at = slice(b * CH, (b + 1) * CH)
            before = x[b * CH - 16 : b * CH, lanes].astype(F32) if b else jnp.zeros((16, CH), F32)
            made = convolve(x[at, lanes].astype(F32), before, factors)
            xc[at, lanes] = made
            part = made.astype(F32) * nn(tokb[at], spreads[:, lanes])
            if b == 0:
                part = jnp.where(iota((CH, CH), 0) >= 3, part, 0.0)
            loaded.append(part.astype(BF16))
        local[:, lanes] = nn(bt[...], jnp.concatenate(loaded, axis=0))

    @pl.loop(0, 4)
    def _(hp):
        local_state(hp)

    pl.semaphore_wait(barrier, ns - 1 + nh - 1)
    tails = [
        pltpu.make_async_remote_copy(
            src_ref=source.at[pl.ds(source.shape[0] - 16, 16)],
            dst_ref=target,
            send_sem=tail_sem.at[2 * i],
            recv_sem=tail_sem.at[2 * i + 1],
            device_id={"seq": lax.rem(me + 1, ns)},
            device_id_type=MESH,
        )
        for i, (source, target) in enumerate(((x, tail_x), (bc, tail_bc)))
    ]
    for copy in tails:
        copy.start()

    @pl.loop(4, 8)
    def _(hp):
        local_state(hp)

    def copy_to(axis, source, target, phase, peer, arrived=None):
        return pltpu.make_async_remote_copy(
            src_ref=source,
            dst_ref=target,
            send_sem=sems.at[2 * phase],
            recv_sem=sems.at[2 * phase + 1] if arrived is None else arrived,
            device_id={axis: peer},
            device_id_type=MESH,
        )

    def wait_all(phase, count, buffer):
        copy_to("seq", buffer.at[pl.ds(0, count)], buffer.at[pl.ds(0, count)], phase, 0).wait_recv()

    def wait_sent(phase, count, buffer):
        copy_to("seq", buffer.at[pl.ds(0, count)], buffer.at[pl.ds(0, count)], phase, 0).wait_send()

    info[...] = jnp.sum(jnp.where(iota((16, CH), 0) == iota((16, CH), 1), logs, 0.0), axis=0, keepdims=True)
    info_all[me] = info[...]

    starts = nn(tokb[0:16], spreads[...])
    for copy in tails:
        copy.wait()
    before_bc = jnp.where(me > 0, tail_bc[...].astype(F32), 0.0)
    conv_bc(0, 16, before_bc)
    first_b = jnp.concatenate([mix[pl.ds(0, 16, stride=2)], jnp.zeros((CH - 16, CH), F32)], axis=0)
    first_b = jnp.transpose(first_b).astype(BF16)[:, :16]
    made = convolve(x[0:16].astype(F32), jnp.where(me > 0, tail_x[...].astype(F32), 0.0), convx[...].astype(F32))
    xc[0:16] = made
    first_x = jnp.where(iota(starts.shape, 0) < 3, made.astype(F32) * starts, 0.0).astype(BF16)
    for hp in range(8):
        lanes = slice(hp * CH, (hp + 1) * CH)
        state = (local[:, lanes] + nn(first_b, first_x[:, lanes])).astype(BF16)
        for a in range(4):
            s_send[hp * 4 + a] = state[32 * a : 32 * a + 32]

    each_seq_peer(lambda peer: copy_to("seq", s_send.at[peer], p1.at[me], 1, peer).start())
    each_seq_peer(lambda peer: copy_to("seq", info, info_all.at[me], 0, peer).start())
    p1[me] = s_send[me]

    for i in (1, 8, 9, 10, 11, 12, 13):
        loads[i].wait()
    conv_bc(0, CH, before_bc)
    turn_b(0)
    for b in range(4):
        at = slice(b * CH, (b + 1) * CH)
        cm[at] = mix[pl.ds(2 * b * CH + 1, CH, stride=2)].astype(BF16)
        paired[b] = jnp.where(iota((CH, CH), 0) >= iota((CH, CH), 1), nn(cm[at], bt[:, at]), 0.0)
        here = cumul[16 * b : 16 * b + 16]
        parts = split2(jnp.exp(here[:, CH - 1 :] - here) * steps[:, at]) + split2(jnp.exp(here)) + split3(here)
        rows = [part.astype(F32) for part in parts] + [jnp.zeros((16, CH), F32)]
        tokc[at] = jnp.transpose(jnp.concatenate(rows, axis=0)).astype(BF16)
        for h in range(16):
            prow[0, h, :, at] = here[h : h + 1]
    for h in range(16):
        prow[1, h] = steps[h : h + 1]
    skip_column = column(skip[...])

    def inside(hp):
        lanes = pl.ds(pl.multiple_of(hp * CH, CH), CH)
        first = iota((CH, CH), 1) < 64
        spread = (codes[...] == 2 * hp).astype(F32).astype(BF16)
        mine = iota((1, CH), 1) // 64 + 2 * hp == iota((16, 1), 0)
        skips = jnp.sum(jnp.where(mine, skip_column, 0.0), axis=0, keepdims=True)
        state = None
        ahead = jnp.ones((1, CH), F32)
        for b in range(4):
            at = slice(b * CH, (b + 1) * CH)
            wide = nn(tokc[at], spread)
            factor, decay = wide[:, :CH], wide[:, CH : 2 * CH]
            pairs = paired[b]
            values = xc[at, lanes]
            halves = []
            for i in range(2):
                later = wide[:, (i + 2) * CH : (i + 3) * CH]
                earlier = prow[0, 2 * hp + i, :, at]
                step = prow[1, 2 * hp + i, :, at]
                halves.append((pairs * jnp.exp(jnp.minimum(later - earlier, 0.0)) * step).astype(BF16))
            zeros = jnp.zeros_like(values)
            blocks = jnp.concatenate([jnp.where(first, values, zeros), jnp.where(first, zeros, values)], axis=0)
            exact = values.astype(F32)
            total = nn(jnp.concatenate(halves, axis=1), blocks) + skips * exact
            if b:
                total = total + decay * sum(nn(cm[at], part) for part in reversed(split2(state)))
            gate = z[at, lanes].astype(F32)
            gate = gate * (0.5 * jnp.tanh(0.5 * gate) + 0.5)
            lg[at, lanes] = total * gate
            eg[at, lanes] = decay * ahead * gate
            if b < 3:
                added = nn(bt[:, at], (exact * factor).astype(BF16))
                state = decay[CH - 1 :] * state + added if b else added
                ahead = ahead * decay[CH - 1 :]

    @pl.loop(0, 5)
    def _(hp):
        inside(hp)

    lane = iota((1, CH), 1)
    spread = (iota((CH, CH), 0) == 2 * (me // 4) + iota((CH, CH), 1) // 64).astype(F32).astype(BF16)
    wait_all(0, ns - 1, info_all)
    decays = jnp.where(lane < 16, jnp.exp(jnp.sum(info_all[...], axis=1)), 0.0)
    decays = sum(nn(part, spread) for part in reversed(split3(decays)))
    wait_all(1, ns - 1, p1)
    entering = jnp.zeros((32, CH), F32)
    for j in range(ns):
        e_send[j] = entering.astype(BF16)
        if j < ns - 1:
            entering = decays[j : j + 1] * entering + p1[j].astype(F32)
    each_seq_peer(lambda peer: copy_to("seq", e_send.at[peer], p2.at[me], 2, peer, p2_sem.at[me]).start())
    p2[me] = e_send[me]

    @pl.loop(5, 8)
    def _(hp):
        inside(hp)

    member[...] = (iota((CH, 4 * CH), 0) == pid[...]).astype(F32).astype(BF16)
    q_send[1:2] = nt(jnp.ones((8, 4 * CH), BF16), member[...])[0:1]
    valid = lane < NP
    ranks = jnp.where(iota((NP, NP), 0) == torder[...], tlogits[...], 0.0)
    ranks = jnp.sum(ranks, axis=1, keepdims=True)
    teacher = jnp.sum(jnp.where(iota((NP, CH), 0) == iota((NP, CH), 1), ranks, 0.0), axis=0, keepdims=True)
    teacher = teacher - jnp.log(jnp.sum(jnp.where(valid, jnp.exp(teacher), 0.0), axis=1, keepdims=True))
    share = jnp.where(valid, jnp.exp(teacher), 0.0)
    weights = weight[...].astype(F32)
    weights = jnp.concatenate([weights[hp : hp + 1] for hp in range(8)], axis=1)
    weights = jnp.broadcast_to(weights, (16, 8 * CH)).astype(BF16)
    gains = gain[...].astype(F32)

    @pl.loop(0, 8)
    def _(i):
        hp = seq_pair(7 - i)
        lanes = pl.ds(pl.multiple_of(hp * CH, CH), CH)
        for a in range(4):
            peer = 4 * hp + a

            @pl.when(peer != me)
            def _():
                copy_to("seq", p2.at[peer], p2.at[peer], 2, peer, p2_sem.at[peer]).wait_recv()

        state = p2[pl.ds(4 * hp, 4)].reshape(CH, CH)
        for b in range(4):
            at = slice(b * CH, (b + 1) * CH)
            gated = lg[at, lanes] + eg[at, lanes] * nn(cm[at], state)
            lg[at, lanes] = gated
            squares[at] += gated * gated

    def store(b):
        at = pl.ds(pl.multiple_of(b * CH, CH), CH)
        return pltpu.make_async_copy(mixed.at[at], result.at[at], out_sem.at[b])

    @pl.loop(0, 4)
    def _(b):
        at = pl.ds(pl.multiple_of(b * CH, CH), CH)
        scale = lax.rsqrt(jnp.sum(squares[at], axis=1, keepdims=True) / (8 * CH) + EPS)
        for hp in range(8):
            lanes = slice(hp * CH, (hp + 1) * CH)
            mixed[at, lanes] = (lg[at, lanes] * scale * gains[hp : hp + 1]).astype(BF16)
        read[b] = nt(weights, mixed[at, :])[0:8]
        store(b).start()

    readout = jnp.concatenate([read[b] for b in range(4)], axis=1)
    part = sum(nt(part, member[...]) for part in reversed(split3(readout)))
    h_send[...] = part[0:1]
    h_all[mh] = part[0:1]
    each_head_peer(lambda peer: copy_to("head", h_send, h_all.at[mh], 3, peer).start())
    wait_all(3, nh - 1, h_all)
    q_send[0:1] = jnp.sum(h_all[...], axis=0)
    q_all[me] = q_send[...]
    each_seq_peer(lambda peer: copy_to("seq", q_send, q_all.at[me], 4, peer).start())
    for b in range(4):
        store(b).wait()
    wait_sent(0, ns - 1, info_all)
    wait_sent(1, ns - 1, s_send)
    wait_sent(2, ns - 1, e_send)
    wait_sent(3, nh - 1, h_all)
    wait_all(4, ns - 1, q_all)
    totals = jnp.sum(q_all[...], axis=0)
    counts = jnp.where(valid, totals[1:2], 1.0)
    squash = jnp.tanh(totals[0:1] / counts / CAP)
    scores = CAP * squash
    student = scores - jnp.log(jnp.sum(jnp.where(valid, jnp.exp(scores), 0.0), axis=1, keepdims=True))
    kl[...] = jnp.sum(share * (teacher - student), axis=1, keepdims=True)
    coef = (jnp.exp(student) - share) * (1.0 - squash * squash) * (4.0 * CH * ns) / counts
    coef = jnp.broadcast_to(jnp.where(valid, coef, 0.0), (8, CH))
    tgrad[...] = sum(nn(part, member[...]) for part in reversed(split3(coef)))[0:1]
    wait_sent(4, ns - 1, q_all)


def solution(mesh):
    ns, nh = mesh.shape["seq"], mesh.shape["head"]

    def per_device(
        x_in, z_in, bc_in, dt_raw, dt_bias, a_log, conv_x, conv_bc, skip_gain, norm_gain, score_weight, passage_ids,
        teacher_logits, teacher_order,
    ):
        vmem = pl.BlockSpec(memory_space=pltpu.VMEM)
        hbm = pl.BlockSpec(memory_space=pltpu.HBM)
        tokens, width = x_in.shape
        given = (
            x_in,
            z_in,
            bc_in.reshape(2 * tokens, CH),
            dt_raw.T,
            dt_bias[None],
            a_log[None],
            conv_x,
            conv_bc.reshape(8, CH),
            skip_gain[None],
            norm_gain.reshape(8, CH),
            score_weight.reshape(8, CH),
            passage_ids[None],
            teacher_logits[None],
            teacher_order[None],
        )
        mixed, tgrad, kl = pl.pallas_call(
            functools.partial(kernel, ns, nh),
            out_shape=(
                jax.ShapeDtypeStruct((tokens, width), BF16),
                jax.ShapeDtypeStruct((1, tokens), F32),
                jax.ShapeDtypeStruct((1, 1), F32),
            ),
            in_specs=[hbm] * 14,
            out_specs=(hbm, vmem, vmem),
            scratch_shapes=[
                *(pltpu.VMEM(array.shape, array.dtype) for array in given),
                pltpu.VMEM((tokens, width), BF16),
                pltpu.VMEM((tokens, CH), BF16),
                pltpu.VMEM((CH, tokens), BF16),
                pltpu.VMEM((2 * tokens, CH), F32),
                pltpu.VMEM((4, CH, CH), F32),
                pltpu.VMEM((tokens, CH), BF16),
                pltpu.VMEM((tokens, CH), BF16),
                pltpu.VMEM((CH, width), BF16),
                pltpu.VMEM((CH, 4 * CH), jnp.int32),
                pltpu.VMEM((CH, width), F32),
                pltpu.VMEM((tokens, width), F32),
                pltpu.VMEM((tokens, width), F32),
                pltpu.VMEM((tokens, CH), F32),
                pltpu.VMEM((4, 8, CH), F32),
                pltpu.VMEM((CH, tokens), BF16),
                pltpu.VMEM((2, 16, 1, tokens), F32),
                pltpu.VMEM((16, width), BF16),
                pltpu.VMEM((16, CH), BF16),
                pltpu.VMEM((1, CH), F32),
                pltpu.VMEM((ns, 1, CH), F32),
                pltpu.VMEM((ns, 32, CH), BF16),
                pltpu.VMEM((ns, 32, CH), BF16),
                pltpu.VMEM((ns, 32, CH), BF16),
                pltpu.VMEM((ns, 32, CH), BF16),
                pltpu.VMEM((1, CH), F32),
                pltpu.VMEM((nh, 1, CH), F32),
                pltpu.VMEM((2, CH), F32),
                pltpu.VMEM((ns, 2, CH), F32),
                pltpu.VMEM((tokens, width), BF16),
                pltpu.SemaphoreType.DMA((14,)),
                pltpu.SemaphoreType.DMA((4,)),
                pltpu.SemaphoreType.DMA((4,)),
                pltpu.SemaphoreType.DMA((10,)),
                pltpu.SemaphoreType.DMA((ns,)),
            ],
            compiler_params=pltpu.CompilerParams(
                collective_id=0, has_side_effects=True, vmem_limit_bytes=63_400_000
            ),
        )(*given)
        return mixed, tgrad.reshape(tokens), kl.reshape(())

    return jax.shard_map(
        per_device,
        mesh=mesh,
        in_specs=(
            P("seq", "head"), P("seq", "head"), P("seq", "head", None, None), P("seq", "head"), P("head"), P("head"),
            P(None, "head"), P(None, "head", None, None), P("head"), P("head"), P("head"), P("seq"), P(), P(),
        ),
        out_specs=(P("seq", "head"), P("seq"), P()),
        check_vma=False,
    )
```

```python
import functools

import jax
import jax.numpy as jnp
from jax import lax
from jax.experimental import pallas as pl
from jax.experimental.pallas import tpu as pltpu
from jax.sharding import PartitionSpec as P

CH = 128
NP = 100
EPS = 1e-05
CAP = 8.0
F32 = jnp.float32
BF16 = jnp.bfloat16
MESH = pl.DeviceIdType.MESH
FAR = (4, 5, 3, 6, 2, 7, 1, 0)
PARTS = 1
PART = 32 // PARTS


def nn(a, b):
    return lax.dot_general(a, b, (((1,), (0,)), ((), ())), preferred_element_type=F32)


def nt(a, b):
    return lax.dot_general(a, b, (((1,), (1,)), ((), ())), preferred_element_type=F32)


def iota(shape, dim):
    return lax.broadcasted_iota(jnp.int32, shape, dim)


def split2(v):
    high = v.astype(BF16)
    return high, (v - high.astype(F32)).astype(BF16)


def split3(v):
    high = v.astype(BF16)
    rest = v - high.astype(F32)
    mid = rest.astype(BF16)
    return high, mid, (rest - mid.astype(F32)).astype(BF16)


def column(row):
    n = row.shape[1]
    return jnp.sum(jnp.where(iota((n, n), 0) == iota((n, n), 1), row, 0.0), axis=1, keepdims=True)


def silu(v):
    below = 1.0 + jnp.exp(-v)
    guess = pl.reciprocal(below, approx=True)
    return v * (guess * (2.0 - below * guess))


def convolve(current, before, taps):
    padded = jnp.concatenate([before, current], axis=0)
    total = jnp.zeros(current.shape, F32)
    for tap in range(4):
        shifted = padded if tap == 3 else pltpu.roll(padded, 3 - tap, 0)
        total = total + shifted[16:] * taps[tap : tap + 1]
    return silu(total).astype(BF16)


def spread_codes(shape, sections):
    row, lane = iota(shape, 0), iota(shape, 1)
    code = jnp.full(shape, -1, jnp.int32)
    for first, last, start, width, size in sections:
        inside = (row >= first) & (row < last) & (lane >= start) & (lane < start + width)
        code = jnp.where(inside, (row & 15) - (lane - start) // size, code)
    return code


def kernel(ns, nh, *refs):
    given, (mixed, tgrad, kl), held = refs[:14], refs[14:17], refs[17:31]
    x, z, bc, dt, bias, alog, convx, convbc, skip, gain, weight, pid, tlogits, torder = held
    (
        xc, cm, bt, mix, paired, tokb, tokc, spreads, codes, local, lg, eg, squares, read, member, prow, tail_x, tail_bc,
        info, info_all, s_send, p1, e_send, p2, h_send, h_all, q_send, q_all,
        in_sem, tail_sem, sems, p2_sem,
    ) = refs[31:]
    me = lax.axis_index("seq")
    mh = lax.axis_index("head")

    def far(i):
        return 4 + (2 * lax.rem(i, 2) - 1) * ((i + 1) // 2)

    def seq_pair(i):
        return lax.rem(me // 4 + far(i), 8)

    def each_seq_peer(act):
        for offset in FAR:
            pair = lax.rem(me // 4 + offset, 8)
            for a in range(4):
                if offset:
                    act(4 * pair + a)
                else:
                    pl.when(4 * pair + a != me)(functools.partial(act, 4 * pair + a))

    def each_head_peer(act):
        for offset in FAR[: nh - 1]:
            act(lax.rem(mh + offset, nh))

    barrier = pltpu.get_barrier_semaphore()
    each_seq_peer(lambda peer: pl.semaphore_signal(barrier, inc=1, device_id={"seq": peer}, device_id_type=MESH))
    each_head_peer(lambda peer: pl.semaphore_signal(barrier, inc=1, device_id={"head": peer}, device_id_type=MESH))

    loads = [
        pltpu.make_async_copy(source, target, in_sem.at[i])
        for i, (source, target) in enumerate(zip(given, held))
    ]
    for i in (3, 4, 5, 2, 7, 0, 6, 11, 1, 8, 9, 10, 12, 13):
        loads[i].start()

    codes[...] = spread_codes((CH, 4 * CH), ((0, 32, 0, CH, 64), (32, 64, CH, CH, 64), (64, 112, 2 * CH, 2 * CH, CH)))
    for hp in range(8):
        code = spread_codes((CH, CH), ((0, 32, 0, CH, 64),))
        spreads[:, hp * CH : (hp + 1) * CH] = (code == 2 * hp).astype(F32).astype(BF16)
    squares[...] = jnp.zeros(squares.shape, F32)

    for i in (3, 4, 5):
        loads[i].wait()
    steps = jax.nn.softplus(dt[...] + column(bias[...]))
    rates = -jnp.exp(column(alog[...])) * steps
    upto = (iota((CH, CH), 0) <= iota((CH, CH), 1)).astype(F32).astype(BF16)
    stacked = jnp.concatenate([rates[:, b * CH : (b + 1) * CH] for b in range(4)], axis=0)
    cumul = sum(nn(part, upto) for part in reversed(split3(stacked)))
    logs = jnp.zeros((16, 1), F32)
    for b in reversed(range(4)):
        here = cumul[16 * b : 16 * b + 16]
        logs = logs + here[:, CH - 1 :]
        parts = split2(jnp.exp(logs - here) * steps[:, b * CH : (b + 1) * CH])
        rows = [part.astype(F32) for part in parts] + [jnp.zeros((96, CH), F32)]
        tokb[b * CH : (b + 1) * CH] = jnp.transpose(jnp.concatenate(rows, axis=0)).astype(BF16)

    even = iota((8, CH), 0) % 2 == 0
    for i in (2, 7):
        loads[i].wait()
    taps = convbc[...].astype(F32)

    def conv_bc(first, count, before):
        current = bc[2 * first : 2 * (first + count)].astype(F32)
        padded = jnp.concatenate([before, current], axis=0)
        total = jnp.zeros((count // 4, 8, CH), F32)
        for tap in range(4):
            shifted = padded if tap == 3 else pltpu.roll(padded, 2 * (3 - tap), 0)
            factor = jnp.where(even, taps[2 * tap : 2 * tap + 1], taps[2 * tap + 1 : 2 * tap + 2])
            total = total + shifted[16:].reshape(count // 4, 8, CH) * factor[None]
        mix[2 * first : 2 * (first + count)] = silu(total).reshape(2 * count, CH)

    def turn_b(b):
        bt[:, b * CH : (b + 1) * CH] = jnp.transpose(mix[pl.ds(2 * b * CH, CH, stride=2)]).astype(BF16)

    for b in range(4):
        conv_bc(b * CH, CH, bc[2 * b * CH - 16 : 2 * b * CH].astype(F32) if b else jnp.zeros((16, CH), F32))
        turn_b(b)
    for i in (0, 6):
        loads[i].wait()

    def local_state(hp):
        lanes = pl.ds(pl.multiple_of(hp * CH, CH), CH)
        factors = convx[:, lanes].astype(F32)
        loaded = []
        for b in range(4):
            at = slice(b * CH, (b + 1) * CH)
            before = x[b * CH - 16 : b * CH, lanes].astype(F32) if b else jnp.zeros((16, CH), F32)
            made = convolve(x[at, lanes].astype(F32), before, factors)
            xc[at, lanes] = made
            part = made.astype(F32) * nn(tokb[at], spreads[:, lanes])
            if b == 0:
                part = jnp.where(iota((CH, CH), 0) >= 3, part, 0.0)
            loaded.append(part.astype(BF16))
        local[:, lanes] = nn(bt[...], jnp.concatenate(loaded, axis=0))

    @pl.loop(0, 4)
    def _(hp):
        local_state(hp)

    pl.semaphore_wait(barrier, ns - 1 + nh - 1)
    tails = [
        pltpu.make_async_remote_copy(
            src_ref=source.at[pl.ds(source.shape[0] - 16, 16)],
            dst_ref=target,
            send_sem=tail_sem.at[2 * i],
            recv_sem=tail_sem.at[2 * i + 1],
            device_id={"seq": lax.rem(me + 1, ns)},
            device_id_type=MESH,
        )
        for i, (source, target) in enumerate(((x, tail_x), (bc, tail_bc)))
    ]
    for copy in tails:
        copy.start()

    @pl.loop(4, 8)
    def _(hp):
        local_state(hp)

    def copy_to(axis, source, target, phase, peer, arrived=None):
        return pltpu.make_async_remote_copy(
            src_ref=source,
            dst_ref=target,
            send_sem=sems.at[2 * phase],
            recv_sem=sems.at[2 * phase + 1] if arrived is None else arrived,
            device_id={axis: peer},
            device_id_type=MESH,
        )

    def wait_all(phase, count, buffer):
        copy_to("seq", buffer.at[pl.ds(0, count)], buffer.at[pl.ds(0, count)], phase, 0).wait_recv()

    def wait_sent(phase, count, buffer):
        copy_to("seq", buffer.at[pl.ds(0, count)], buffer.at[pl.ds(0, count)], phase, 0).wait_send()

    info[...] = jnp.sum(jnp.where(iota((16, CH), 0) == iota((16, CH), 1), logs, 0.0), axis=0, keepdims=True)
    info_all[me] = info[...]

    starts = nn(tokb[0:16], spreads[...])
    for copy in tails:
        copy.wait()
    before_bc = jnp.where(me > 0, tail_bc[...].astype(F32), 0.0)
    conv_bc(0, 16, before_bc)
    first_b = jnp.concatenate([mix[pl.ds(0, 16, stride=2)], jnp.zeros((CH - 16, CH), F32)], axis=0)
    first_b = jnp.transpose(first_b).astype(BF16)[:, :16]
    made = convolve(x[0:16].astype(F32), jnp.where(me > 0, tail_x[...].astype(F32), 0.0), convx[...].astype(F32))
    xc[0:16] = made
    first_x = jnp.where(iota(starts.shape, 0) < 3, made.astype(F32) * starts, 0.0).astype(BF16)
    for hp in range(8):
        lanes = slice(hp * CH, (hp + 1) * CH)
        state = (local[:, lanes] + nn(first_b, first_x[:, lanes])).astype(BF16)
        for a in range(4):
            for q in range(PARTS):
                s_send[q, hp * 4 + a] = state[32 * a + PART * q : 32 * a + PART * (q + 1)]

    def send_states(q):
        each_seq_peer(lambda peer: copy_to("seq", s_send.at[q, peer], p1.at[q, me], 3 + q, peer).start())
        p1[q, me] = s_send[q, me]

    send_states(0)
    each_seq_peer(lambda peer: copy_to("seq", info, info_all.at[me], 0, peer).start())
    for q in range(1, PARTS):
        send_states(q)

    for i in (1, 8, 9, 10, 11, 12, 13):
        loads[i].wait()
    conv_bc(0, CH, before_bc)
    turn_b(0)
    for b in range(4):
        at = slice(b * CH, (b + 1) * CH)
        cm[at] = mix[pl.ds(2 * b * CH + 1, CH, stride=2)].astype(BF16)
        paired[b] = jnp.where(iota((CH, CH), 0) >= iota((CH, CH), 1), nn(cm[at], bt[:, at]), 0.0)
        here = cumul[16 * b : 16 * b + 16]
        parts = split2(jnp.exp(here[:, CH - 1 :] - here) * steps[:, at]) + split2(jnp.exp(here)) + split3(here)
        rows = [part.astype(F32) for part in parts] + [jnp.zeros((16, CH), F32)]
        tokc[at] = jnp.transpose(jnp.concatenate(rows, axis=0)).astype(BF16)
        for h in range(16):
            prow[0, h, :, at] = here[h : h + 1]
    for h in range(16):
        prow[1, h] = steps[h : h + 1]
    skip_column = column(skip[...])

    def inside(hp):
        lanes = pl.ds(pl.multiple_of(hp * CH, CH), CH)
        first = iota((CH, CH), 1) < 64
        spread = (codes[...] == 2 * hp).astype(F32).astype(BF16)
        mine = iota((1, CH), 1) // 64 + 2 * hp == iota((16, 1), 0)
        skips = jnp.sum(jnp.where(mine, skip_column, 0.0), axis=0, keepdims=True)
        state = None
        ahead = jnp.ones((1, CH), F32)
        for b in range(4):
            at = slice(b * CH, (b + 1) * CH)
            wide = nn(tokc[at], spread)
            factor, decay = wide[:, :CH], wide[:, CH : 2 * CH]
            pairs = paired[b]
            values = xc[at, lanes]
            halves = []
            for i in range(2):
                later = wide[:, (i + 2) * CH : (i + 3) * CH]
                earlier = prow[0, 2 * hp + i, :, at]
                step = prow[1, 2 * hp + i, :, at]
                halves.append((pairs * jnp.exp(jnp.minimum(later - earlier, 0.0)) * step).astype(BF16))
            zeros = jnp.zeros_like(values)
            blocks = jnp.concatenate([jnp.where(first, values, zeros), jnp.where(first, zeros, values)], axis=0)
            exact = values.astype(F32)
            total = nn(jnp.concatenate(halves, axis=1), blocks) + skips * exact
            if b:
                total = total + decay * sum(nn(cm[at], part) for part in reversed(split2(state)))
            gate = z[at, lanes].astype(F32)
            gate = gate * (0.5 * jnp.tanh(0.5 * gate) + 0.5)
            lg[at, lanes] = total * gate
            eg[at, lanes] = decay * ahead * gate
            if b < 3:
                added = nn(bt[:, at], (exact * factor).astype(BF16))
                state = decay[CH - 1 :] * state + added if b else added
                ahead = ahead * decay[CH - 1 :]

    @pl.loop(0, 5)
    def _(hp):
        inside(hp)

    lane = iota((1, CH), 1)
    spread = (iota((CH, CH), 0) == 2 * (me // 4) + iota((CH, CH), 1) // 64).astype(F32).astype(BF16)
    wait_all(0, ns - 1, info_all)
    decays = jnp.where(lane < 16, jnp.exp(jnp.sum(info_all[...], axis=1)), 0.0)
    decays = sum(nn(part, spread) for part in reversed(split3(decays)))

    def send_entering(q):
        def act(peer):
            arrived = p2_sem.at[q, me]
            copy_to("seq", e_send.at[q, peer], p2.at[me, pl.ds(PART * q, PART)], 3 + PARTS + q, peer, arrived).start()

        wait_all(3 + q, ns - 1, p1.at[q])
        entering = jnp.zeros((PART, CH), F32)
        for j in range(ns):
            e_send[q, j] = entering.astype(BF16)
            if j < ns - 1:
                entering = decays[j : j + 1] * entering + p1[q, j].astype(F32)
        each_seq_peer(act)
        p2[me, PART * q : PART * (q + 1)] = e_send[q, me]

    for q in range(PARTS):
        send_entering(q)

    @pl.loop(5, 8)
    def _(hp):
        inside(hp)

    member[...] = (iota((CH, 4 * CH), 0) == pid[...]).astype(F32).astype(BF16)
    q_send[1:2] = nt(jnp.ones((8, 4 * CH), BF16), member[...])[0:1]
    valid = lane < NP
    ranks = jnp.where(iota((NP, NP), 0) == torder[...], tlogits[...], 0.0)
    ranks = jnp.sum(ranks, axis=1, keepdims=True)
    teacher = jnp.sum(jnp.where(iota((NP, CH), 0) == iota((NP, CH), 1), ranks, 0.0), axis=0, keepdims=True)
    teacher = teacher - jnp.log(jnp.sum(jnp.where(valid, jnp.exp(teacher), 0.0), axis=1, keepdims=True))
    share = jnp.where(valid, jnp.exp(teacher), 0.0)
    weights = weight[...].astype(F32)
    gains = gain[...].astype(F32)

    @pl.loop(0, 8)
    def _(i):
        hp = seq_pair(i)
        lanes = pl.ds(pl.multiple_of(hp * CH, CH), CH)
        for a in range(4):
            peer = 4 * hp + a

            @pl.when(peer != me)
            def _():
                for q in range(PARTS):
                    piece = p2.at[peer, pl.ds(PART * q, PART)]
                    copy_to("seq", piece, piece, 0, peer, p2_sem.at[q, peer]).wait_recv()

        state = p2[pl.ds(4 * hp, 4)].reshape(CH, CH)
        for b in range(4):
            at = slice(b * CH, (b + 1) * CH)
            gated = lg[at, lanes] + eg[at, lanes] * nn(cm[at], state)
            lg[at, lanes] = gated
            squares[at] += gated * gated

    ones = jnp.ones((16, CH), BF16)
    for b in range(4):
        at = slice(b * CH, (b + 1) * CH)
        scale = lax.rsqrt(jnp.sum(squares[at], axis=1, keepdims=True) / (8 * CH) + EPS)
        for hp in range(8):
            lanes = slice(hp * CH, (hp + 1) * CH)
            made = (lg[at, lanes] * scale * gains[hp : hp + 1]).astype(BF16)
            mixed[at, lanes] = made
            term = made.astype(F32) * weights[hp : hp + 1]
            total = total + term if hp else term
        read[b] = sum(nt(ones, part) for part in reversed(split3(total)))[0:8]

    readout = jnp.concatenate([read[b] for b in range(4)], axis=1)
    part = sum(nt(part, member[...]) for part in reversed(split3(readout)))
    h_send[...] = part[0:1]
    h_all[mh] = part[0:1]
    each_head_peer(lambda peer: copy_to("head", h_send, h_all.at[mh], 1, peer).start())
    wait_all(1, nh - 1, h_all)
    q_send[0:1] = jnp.sum(h_all[...], axis=0)
    q_all[me] = q_send[...]
    each_seq_peer(lambda peer: copy_to("seq", q_send, q_all.at[me], 2, peer).start())
    wait_sent(0, ns - 1, info_all)
    for q in range(PARTS):
        wait_sent(3 + q, ns - 1, s_send.at[q])
        wait_sent(3 + PARTS + q, ns - 1, e_send.at[q])
    wait_sent(1, nh - 1, h_all)
    wait_all(2, ns - 1, q_all)
    totals = jnp.sum(q_all[...], axis=0)
    counts = jnp.where(valid, totals[1:2], 1.0)
    squash = jnp.tanh(totals[0:1] / counts / CAP)
    scores = CAP * squash
    student = scores - jnp.log(jnp.sum(jnp.where(valid, jnp.exp(scores), 0.0), axis=1, keepdims=True))
    kl[...] = jnp.sum(share * (teacher - student), axis=1, keepdims=True)
    coef = (jnp.exp(student) - share) * (1.0 - squash * squash) * (4.0 * CH * ns) / counts
    coef = jnp.broadcast_to(jnp.where(valid, coef, 0.0), (8, CH))
    tgrad[...] = sum(nn(part, member[...]) for part in reversed(split3(coef)))[0:1]
    wait_sent(2, ns - 1, q_all)


def solution(mesh):
    ns, nh = mesh.shape["seq"], mesh.shape["head"]

    def per_device(
        x_in, z_in, bc_in, dt_raw, dt_bias, a_log, conv_x, conv_bc, skip_gain, norm_gain, score_weight, passage_ids,
        teacher_logits, teacher_order,
    ):
        vmem = pl.BlockSpec(memory_space=pltpu.VMEM)
        hbm = pl.BlockSpec(memory_space=pltpu.HBM)
        tokens, width = x_in.shape
        given = (
            x_in,
            z_in,
            bc_in.reshape(2 * tokens, CH),
            dt_raw.T,
            dt_bias[None],
            a_log[None],
            conv_x,
            conv_bc.reshape(8, CH),
            skip_gain[None],
            norm_gain.reshape(8, CH),
            score_weight.reshape(8, CH),
            passage_ids[None],
            teacher_logits[None],
            teacher_order[None],
        )
        mixed, tgrad, kl = pl.pallas_call(
            functools.partial(kernel, ns, nh),
            out_shape=(
                pltpu.VMEM((tokens, width), BF16),
                pltpu.VMEM((1, tokens), F32),
                jax.ShapeDtypeStruct((1, 1), F32),
            ),
            in_specs=[hbm] * 14,
            out_specs=(vmem, vmem, vmem),
            scratch_shapes=[
                *(pltpu.VMEM(array.shape, array.dtype) for array in given),
                pltpu.VMEM((tokens, width), BF16),
                pltpu.VMEM((tokens, CH), BF16),
                pltpu.VMEM((CH, tokens), BF16),
                pltpu.VMEM((2 * tokens, CH), F32),
                pltpu.VMEM((4, CH, CH), F32),
                pltpu.VMEM((tokens, CH), BF16),
                pltpu.VMEM((tokens, CH), BF16),
                pltpu.VMEM((CH, width), BF16),
                pltpu.VMEM((CH, 4 * CH), jnp.int32),
                pltpu.VMEM((CH, width), F32),
                pltpu.VMEM((tokens, width), F32),
                pltpu.VMEM((tokens, width), F32),
                pltpu.VMEM((tokens, CH), F32),
                pltpu.VMEM((4, 8, CH), F32),
                pltpu.VMEM((CH, tokens), BF16),
                pltpu.VMEM((2, 16, 1, tokens), F32),
                pltpu.VMEM((16, width), BF16),
                pltpu.VMEM((16, CH), BF16),
                pltpu.VMEM((1, CH), F32),
                pltpu.VMEM((ns, 1, CH), F32),
                pltpu.VMEM((PARTS, ns, PART, CH), BF16),
                pltpu.VMEM((PARTS, ns, PART, CH), BF16),
                pltpu.VMEM((PARTS, ns, PART, CH), BF16),
                pltpu.VMEM((ns, 32, CH), BF16),
                pltpu.VMEM((1, CH), F32),
                pltpu.VMEM((nh, 1, CH), F32),
                pltpu.VMEM((2, CH), F32),
                pltpu.VMEM((ns, 2, CH), F32),
                pltpu.SemaphoreType.DMA((14,)),
                pltpu.SemaphoreType.DMA((4,)),
                pltpu.SemaphoreType.DMA((2 * (3 + 2 * PARTS),)),
                pltpu.SemaphoreType.DMA((PARTS, ns)),
            ],
            compiler_params=pltpu.CompilerParams(
                collective_id=0, has_side_effects=True, vmem_limit_bytes=40 * 2**20
            ),
        )(*(pltpu.with_memory_space_constraint(array, pltpu.HBM) for array in given))
        return mixed, tgrad.reshape(tokens), kl.reshape(())

    return jax.shard_map(
        per_device,
        mesh=mesh,
        in_specs=(
            P("seq", "head"), P("seq", "head"), P("seq", "head", None, None), P("seq", "head"), P("head"), P("head"),
            P(None, "head"), P(None, "head", None, None), P("head"), P("head"), P("head"), P("seq"), P(), P(),
        ),
        out_specs=(P("seq", "head"), P("seq"), P()),
        check_vma=False,
    )
```

```python
import functools

import jax
import jax.numpy as jnp
from jax import lax
from jax.experimental import pallas as pl
from jax.experimental.pallas import tpu as pltpu
from jax.sharding import PartitionSpec as P

CH = 128
NP = 100
EPS = 1e-05
CAP = 8.0
F32 = jnp.float32
BF16 = jnp.bfloat16
MESH = pl.DeviceIdType.MESH
FAR = (4, 5, 3, 6, 2, 7, 1)
NX, NZ = 4, 8
SHIFTS = sorted(
    ((dx, dz) for dx in range(NX) for dz in range(NZ) if dx or dz),
    key=lambda shift: -min(shift[0], NX - shift[0]) - min(shift[1], NZ - shift[1]),
)
PARTS = 1
PART = 32 // PARTS


def nn(a, b):
    return lax.dot_general(a, b, (((1,), (0,)), ((), ())), preferred_element_type=F32)


def nt(a, b):
    return lax.dot_general(a, b, (((1,), (1,)), ((), ())), preferred_element_type=F32)


def iota(shape, dim):
    return lax.broadcasted_iota(jnp.int32, shape, dim)


def split2(v):
    high = v.astype(BF16)
    return high, (v - high.astype(F32)).astype(BF16)


def split3(v):
    high = v.astype(BF16)
    rest = v - high.astype(F32)
    mid = rest.astype(BF16)
    return high, mid, (rest - mid.astype(F32)).astype(BF16)


def column(row):
    n = row.shape[1]
    return jnp.sum(jnp.where(iota((n, n), 0) == iota((n, n), 1), row, 0.0), axis=1, keepdims=True)


def silu(v):
    below = 1.0 + jnp.exp(-v)
    guess = pl.reciprocal(below, approx=True)
    return v * (guess * (2.0 - below * guess))


def convolve(current, before, taps):
    padded = jnp.concatenate([before, current], axis=0)
    total = jnp.zeros(current.shape, F32)
    for tap in range(4):
        shifted = padded if tap == 3 else pltpu.roll(padded, 3 - tap, 0)
        total = total + shifted[16:] * taps[tap : tap + 1]
    return silu(total).astype(BF16)


def spread_codes(shape, sections):
    row, lane = iota(shape, 0), iota(shape, 1)
    code = jnp.full(shape, -1, jnp.int32)
    for first, last, start, width, size in sections:
        inside = (row >= first) & (row < last) & (lane >= start) & (lane < start + width)
        code = jnp.where(inside, (row & 15) - (lane - start) // size, code)
    return code


def kernel(ns, nh, *refs):
    given, (mixed, tgrad, kl), held = refs[:14], refs[14:17], refs[17:31]
    x, z, bc, dt, bias, alog, convx, convbc, skip, gain, weight, pid, tlogits, torder = held
    (
        xc, cm, bt, mix, paired, tokb, tokc, spreads, codes, local, lg, eg, squares, scored, both, member, prow, tail_x, tail_bc,
        info, info_all, s_send, p1, e_send, p2, h_send, h_all, q_send, q_all,
        in_sem, tail_sem, sems, p2_sem,
    ) = refs[31:]
    me = lax.axis_index("seq")
    mh = lax.axis_index("head")

    def far(i):
        return 4 + (2 * lax.rem(i, 2) - 1) * ((i + 1) // 2)

    def seq_pair(i):
        return lax.rem(me // 4 + far(i), 8)

    def each_seq_peer(act):
        for dx, dz in SHIFTS:
            act(lax.rem(me // NZ + dx, NX) * NZ + lax.rem(lax.rem(me, NZ) + dz, NZ))

    def each_head_peer(act):
        for offset in FAR:
            act(lax.rem(mh + offset, nh))

    barrier = pltpu.get_barrier_semaphore()
    each_seq_peer(lambda peer: pl.semaphore_signal(barrier, inc=1, device_id={"seq": peer}, device_id_type=MESH))
    each_head_peer(lambda peer: pl.semaphore_signal(barrier, inc=1, device_id={"head": peer}, device_id_type=MESH))

    loads = [
        pltpu.make_async_copy(source, target, in_sem.at[i])
        for i, (source, target) in enumerate(zip(given, held))
    ]
    for i in (3, 4, 5, 2, 7, 0, 6, 11, 1, 8, 9, 10, 12, 13):
        loads[i].start()

    codes[...] = spread_codes((CH, 4 * CH), ((0, 32, 0, CH, 64), (32, 64, CH, CH, 64), (64, 112, 2 * CH, 2 * CH, CH)))
    for hp in range(8):
        code = spread_codes((CH, CH), ((0, 32, 0, CH, 64),))
        spreads[:, hp * CH : (hp + 1) * CH] = (code == 2 * hp).astype(F32).astype(BF16)
    squares[...] = jnp.zeros(squares.shape, F32)
    scored[...] = jnp.zeros(scored.shape, F32)

    for i in (3, 4, 5):
        loads[i].wait()
    steps = jax.nn.softplus(dt[...] + column(bias[...]))
    rates = -jnp.exp(column(alog[...])) * steps
    upto = (iota((CH, CH), 0) <= iota((CH, CH), 1)).astype(F32).astype(BF16)
    stacked = jnp.concatenate([rates[:, b * CH : (b + 1) * CH] for b in range(4)], axis=0)
    cumul = sum(nn(part, upto) for part in reversed(split3(stacked)))
    logs = jnp.zeros((16, 1), F32)
    for b in reversed(range(4)):
        here = cumul[16 * b : 16 * b + 16]
        logs = logs + here[:, CH - 1 :]
        parts = split2(jnp.exp(logs - here) * steps[:, b * CH : (b + 1) * CH])
        rows = [part.astype(F32) for part in parts] + [jnp.zeros((96, CH), F32)]
        tokb[b * CH : (b + 1) * CH] = jnp.transpose(jnp.concatenate(rows, axis=0)).astype(BF16)

    even = iota((8, CH), 0) % 2 == 0
    for i in (2, 7):
        loads[i].wait()
    taps = convbc[...].astype(F32)

    def conv_bc(first, count, before):
        current = bc[2 * first : 2 * (first + count)].astype(F32)
        padded = jnp.concatenate([before, current], axis=0)
        total = jnp.zeros((count // 4, 8, CH), F32)
        for tap in range(4):
            shifted = padded if tap == 3 else pltpu.roll(padded, 2 * (3 - tap), 0)
            factor = jnp.where(even, taps[2 * tap : 2 * tap + 1], taps[2 * tap + 1 : 2 * tap + 2])
            total = total + shifted[16:].reshape(count // 4, 8, CH) * factor[None]
        mix[2 * first : 2 * (first + count)] = silu(total).reshape(2 * count, CH)

    def turn_b(b):
        bt[:, b * CH : (b + 1) * CH] = jnp.transpose(mix[pl.ds(2 * b * CH, CH, stride=2)]).astype(BF16)

    for b in range(4):
        conv_bc(b * CH, CH, bc[2 * b * CH - 16 : 2 * b * CH].astype(F32) if b else jnp.zeros((16, CH), F32))
        turn_b(b)
    for i in (0, 6):
        loads[i].wait()

    def local_state(hp):
        lanes = pl.ds(pl.multiple_of(hp * CH, CH), CH)
        factors = convx[:, lanes].astype(F32)
        loaded = []
        for b in range(4):
            at = slice(b * CH, (b + 1) * CH)
            before = x[b * CH - 16 : b * CH, lanes].astype(F32) if b else jnp.zeros((16, CH), F32)
            made = convolve(x[at, lanes].astype(F32), before, factors)
            xc[at, lanes] = made
            part = made.astype(F32) * nn(tokb[at], spreads[:, lanes])
            if b == 0:
                part = jnp.where(iota((CH, CH), 0) >= 3, part, 0.0)
            loaded.append(part.astype(BF16))
        local[:, lanes] = nn(bt[...], jnp.concatenate(loaded, axis=0))

    @pl.loop(0, 4)
    def _(hp):
        local_state(hp)

    pl.semaphore_wait(barrier, ns - 1 + nh - 1)
    tails = [
        pltpu.make_async_remote_copy(
            src_ref=source.at[pl.ds(source.shape[0] - 16, 16)],
            dst_ref=target,
            send_sem=tail_sem.at[2 * i],
            recv_sem=tail_sem.at[2 * i + 1],
            device_id={"seq": lax.rem(me + 1, ns)},
            device_id_type=MESH,
        )
        for i, (source, target) in enumerate(((x, tail_x), (bc, tail_bc)))
    ]
    for copy in tails:
        copy.start()

    @pl.loop(4, 8)
    def _(hp):
        local_state(hp)

    def copy_to(axis, source, target, phase, peer, arrived=None):
        return pltpu.make_async_remote_copy(
            src_ref=source,
            dst_ref=target,
            send_sem=sems.at[2 * phase],
            recv_sem=sems.at[2 * phase + 1] if arrived is None else arrived,
            device_id={axis: peer},
            device_id_type=MESH,
        )

    def wait_all(phase, count, buffer):
        copy_to("seq", buffer.at[pl.ds(0, count)], buffer.at[pl.ds(0, count)], phase, 0).wait_recv()

    def wait_sent(phase, count, buffer):
        copy_to("seq", buffer.at[pl.ds(0, count)], buffer.at[pl.ds(0, count)], phase, 0).wait_send()

    info[...] = jnp.sum(jnp.where(iota((16, CH), 0) == iota((16, CH), 1), logs, 0.0), axis=0, keepdims=True)
    info_all[me] = info[...]
    each_seq_peer(lambda peer: copy_to("seq", info, info_all.at[me], 0, peer).start())

    starts = nn(tokb[0:16], spreads[...])
    for copy in tails:
        copy.wait()
    before_bc = jnp.where(me > 0, tail_bc[...].astype(F32), 0.0)
    conv_bc(0, 16, before_bc)
    first_b = jnp.concatenate([mix[pl.ds(0, 16, stride=2)], jnp.zeros((CH - 16, CH), F32)], axis=0)
    first_b = jnp.transpose(first_b).astype(BF16)[:, :16]
    made = convolve(x[0:16].astype(F32), jnp.where(me > 0, tail_x[...].astype(F32), 0.0), convx[...].astype(F32))
    xc[0:16] = made
    first_x = jnp.where(iota(starts.shape, 0) < 3, made.astype(F32) * starts, 0.0).astype(BF16)
    for hp in range(8):
        lanes = slice(hp * CH, (hp + 1) * CH)
        state = (local[:, lanes] + nn(first_b, first_x[:, lanes])).astype(BF16)
        for a in range(4):
            for q in range(PARTS):
                s_send[q, hp * 4 + a] = state[32 * a + PART * q : 32 * a + PART * (q + 1)]

    def send_states(q):
        each_seq_peer(lambda peer: copy_to("seq", s_send.at[q, peer], p1.at[q, me], 3 + q, peer).start())
        p1[q, me] = s_send[q, me]

    send_states(0)
    for q in range(1, PARTS):
        send_states(q)

    for i in (1, 8, 9, 10, 11, 12, 13):
        loads[i].wait()
    conv_bc(0, CH, before_bc)
    turn_b(0)
    for b in range(4):
        at = slice(b * CH, (b + 1) * CH)
        cm[at] = mix[pl.ds(2 * b * CH + 1, CH, stride=2)].astype(BF16)
        paired[b] = jnp.where(iota((CH, CH), 0) >= iota((CH, CH), 1), nn(cm[at], bt[:, at]), 0.0)
        here = cumul[16 * b : 16 * b + 16]
        parts = split2(jnp.exp(here[:, CH - 1 :] - here) * steps[:, at]) + split2(jnp.exp(here)) + split3(here)
        rows = [part.astype(F32) for part in parts] + [jnp.zeros((16, CH), F32)]
        tokc[at] = jnp.transpose(jnp.concatenate(rows, axis=0)).astype(BF16)
        for h in range(16):
            prow[0, h, :, at] = here[h : h + 1]
    for h in range(16):
        prow[1, h] = steps[h : h + 1]
    skip_column = column(skip[...])

    def inside(hp):
        lanes = pl.ds(pl.multiple_of(hp * CH, CH), CH)
        first = iota((CH, CH), 1) < 64
        spread = (codes[...] == 2 * hp).astype(F32).astype(BF16)
        mine = iota((1, CH), 1) // 64 + 2 * hp == iota((16, 1), 0)
        skips = jnp.sum(jnp.where(mine, skip_column, 0.0), axis=0, keepdims=True)
        state = None
        ahead = jnp.ones((1, CH), F32)
        for b in range(4):
            at = slice(b * CH, (b + 1) * CH)
            wide = nn(tokc[at], spread)
            factor, decay = wide[:, :CH], wide[:, CH : 2 * CH]
            pairs = paired[b]
            values = xc[at, lanes]
            halves = []
            for i in range(2):
                later = wide[:, (i + 2) * CH : (i + 3) * CH]
                earlier = prow[0, 2 * hp + i, :, at]
                step = prow[1, 2 * hp + i, :, at]
                halves.append((pairs * jnp.exp(jnp.minimum(later - earlier, 0.0)) * step).astype(BF16))
            zeros = jnp.zeros_like(values)
            blocks = jnp.concatenate([jnp.where(first, values, zeros), jnp.where(first, zeros, values)], axis=0)
            exact = values.astype(F32)
            total = nn(jnp.concatenate(halves, axis=1), blocks) + skips * exact
            if b:
                total = total + decay * sum(nn(cm[at], part) for part in reversed(split2(state)))
            gate = z[at, lanes].astype(F32)
            gate = gate * (0.5 * jnp.tanh(0.5 * gate) + 0.5)
            lg[at, lanes] = total * gate
            eg[at, lanes] = decay * ahead * gate
            if b < 3:
                added = nn(bt[:, at], (exact * factor).astype(BF16))
                state = decay[CH - 1 :] * state + added if b else added
                ahead = ahead * decay[CH - 1 :]

    @pl.loop(0, 5)
    def _(hp):
        inside(hp)

    lane = iota((1, CH), 1)
    spread = (iota((CH, CH), 0) == 2 * (me // 4) + iota((CH, CH), 1) // 64).astype(F32).astype(BF16)
    wait_all(0, ns - 1, info_all)
    decays = jnp.where(lane < 16, jnp.exp(jnp.sum(info_all[...], axis=1)), 0.0)
    decays = sum(nn(part, spread) for part in reversed(split3(decays)))

    def send_entering(q):
        def act(peer):
            arrived = p2_sem.at[q, me]
            copy_to("seq", e_send.at[q, peer], p2.at[me, pl.ds(PART * q, PART)], 3 + PARTS + q, peer, arrived).start()

        wait_all(3 + q, ns - 1, p1.at[q])
        entering = jnp.zeros((PART, CH), F32)
        for j in range(ns):
            e_send[q, j] = entering.astype(BF16)
            if j < ns - 1:
                entering = decays[j : j + 1] * entering + p1[q, j].astype(F32)
        each_seq_peer(act)
        p2[me, PART * q : PART * (q + 1)] = e_send[q, me]

    for q in range(PARTS):
        send_entering(q)

    @pl.loop(5, 8)
    def _(hp):
        inside(hp)

    member[...] = (iota((CH, 4 * CH), 0) == pid[...]).astype(F32).astype(BF16)
    q_send[1:2] = nt(jnp.ones((8, 4 * CH), BF16), member[...])[0:1]
    valid = lane < NP
    ranks = jnp.where(iota((NP, NP), 0) == torder[...], tlogits[...], 0.0)
    ranks = jnp.sum(ranks, axis=1, keepdims=True)
    teacher = jnp.sum(jnp.where(iota((NP, CH), 0) == iota((NP, CH), 1), ranks, 0.0), axis=0, keepdims=True)
    teacher = teacher - jnp.log(jnp.sum(jnp.where(valid, jnp.exp(teacher), 0.0), axis=1, keepdims=True))
    share = jnp.where(valid, jnp.exp(teacher), 0.0)
    gains = gain[...].astype(F32)
    products = gains * weight[...].astype(F32)
    for hp in range(8):
        both[hp] = products[hp : hp + 1]

    @pl.loop(0, 4)
    def _(step):
        pairs = [seq_pair(2 * step + i) for i in range(2)]
        for hp in pairs:
            for a in range(4):
                peer = 4 * hp + a

                @pl.when(peer != me)
                def _():
                    for q in range(PARTS):
                        piece = p2.at[peer, pl.ds(PART * q, PART)]
                        copy_to("seq", piece, piece, 0, peer, p2_sem.at[q, peer]).wait_recv()

        for b in range(4):
            at = slice(b * CH, (b + 1) * CH)
            power, score = squares[at], scored[at]
            for hp in pairs:
                lanes = pl.ds(pl.multiple_of(hp * CH, CH), CH)
                state = p2[pl.ds(4 * hp, 4)].reshape(CH, CH)
                gated = lg[at, lanes] + eg[at, lanes] * nn(cm[at], state)
                lg[at, lanes] = gated
                power = power + gated * gated
                score = score + gated * both[hp]
            squares[at], scored[at] = power, score

    ones = jnp.ones((16, CH), BF16)
    readout = []
    for b in range(4):
        at = slice(b * CH, (b + 1) * CH)
        power = sum(nt(ones, part) for part in reversed(split3(squares[at])))[0:8]
        plain = sum(nt(ones, part) for part in reversed(split3(scored[at])))[0:8]
        readout.append(plain * lax.rsqrt(power / (8 * CH) + EPS))
    part = sum(nt(part, member[...]) for part in reversed(split3(jnp.concatenate(readout, axis=1))))
    h_send[...] = part[0:1]
    h_all[mh] = part[0:1]
    each_head_peer(lambda peer: copy_to("head", h_send, h_all.at[mh], 1, peer).start())

    for b in range(4):
        at = slice(b * CH, (b + 1) * CH)
        scale = lax.rsqrt(jnp.sum(squares[at], axis=1, keepdims=True) / (8 * CH) + EPS)
        for hp in range(8):
            lanes = slice(hp * CH, (hp + 1) * CH)
            mixed[at, lanes] = (lg[at, lanes] * scale * gains[hp : hp + 1]).astype(BF16)
    wait_all(1, nh - 1, h_all)
    q_send[0:1] = jnp.sum(h_all[...], axis=0)
    q_all[me] = q_send[...]
    each_seq_peer(lambda peer: copy_to("seq", q_send, q_all.at[me], 2, peer).start())
    wait_sent(0, ns - 1, info_all)
    for q in range(PARTS):
        wait_sent(3 + q, ns - 1, s_send.at[q])
        wait_sent(3 + PARTS + q, ns - 1, e_send.at[q])
    wait_sent(1, nh - 1, h_all)
    wait_all(2, ns - 1, q_all)
    totals = jnp.sum(q_all[...], axis=0)
    counts = jnp.where(valid, totals[1:2], 1.0)
    squash = jnp.tanh(totals[0:1] / counts / CAP)
    scores = CAP * squash
    student = scores - jnp.log(jnp.sum(jnp.where(valid, jnp.exp(scores), 0.0), axis=1, keepdims=True))
    kl[...] = jnp.sum(share * (teacher - student), axis=1, keepdims=True)
    coef = (jnp.exp(student) - share) * (1.0 - squash * squash) * (4.0 * CH * ns) / counts
    coef = jnp.broadcast_to(jnp.where(valid, coef, 0.0), (8, CH))
    tgrad[...] = sum(nn(part, member[...]) for part in reversed(split3(coef)))[0:1]
    wait_sent(2, ns - 1, q_all)


def solution(mesh):
    ns, nh = mesh.shape["seq"], mesh.shape["head"]

    def per_device(
        x_in, z_in, bc_in, dt_raw, dt_bias, a_log, conv_x, conv_bc, skip_gain, norm_gain, score_weight, passage_ids,
        teacher_logits, teacher_order,
    ):
        vmem = pl.BlockSpec(memory_space=pltpu.VMEM)
        hbm = pl.BlockSpec(memory_space=pltpu.HBM)
        tokens, width = x_in.shape
        given = (
            x_in,
            z_in,
            bc_in.reshape(2 * tokens, CH),
            dt_raw.T,
            dt_bias[None],
            a_log[None],
            conv_x,
            conv_bc.reshape(8, CH),
            skip_gain[None],
            norm_gain.reshape(8, CH),
            score_weight.reshape(8, CH),
            passage_ids[None],
            teacher_logits[None],
            teacher_order[None],
        )
        mixed, tgrad, kl = pl.pallas_call(
            functools.partial(kernel, ns, nh),
            out_shape=(
                pltpu.VMEM((tokens, width), BF16),
                pltpu.VMEM((1, tokens), F32),
                jax.ShapeDtypeStruct((1, 1), F32),
            ),
            in_specs=[hbm] * 14,
            out_specs=(vmem, vmem, vmem),
            scratch_shapes=[
                *(pltpu.VMEM(array.shape, array.dtype) for array in given),
                pltpu.VMEM((tokens, width), BF16),
                pltpu.VMEM((tokens, CH), BF16),
                pltpu.VMEM((CH, tokens), BF16),
                pltpu.VMEM((2 * tokens, CH), F32),
                pltpu.VMEM((4, CH, CH), F32),
                pltpu.VMEM((tokens, CH), BF16),
                pltpu.VMEM((tokens, CH), BF16),
                pltpu.VMEM((CH, width), BF16),
                pltpu.VMEM((CH, 4 * CH), jnp.int32),
                pltpu.VMEM((CH, width), F32),
                pltpu.VMEM((tokens, width), F32),
                pltpu.VMEM((tokens, width), F32),
                pltpu.VMEM((tokens, CH), F32),
                pltpu.VMEM((tokens, CH), F32),
                pltpu.VMEM((8, 1, CH), F32),
                pltpu.VMEM((CH, tokens), BF16),
                pltpu.VMEM((2, 16, 1, tokens), F32),
                pltpu.VMEM((16, width), BF16),
                pltpu.VMEM((16, CH), BF16),
                pltpu.VMEM((1, CH), F32),
                pltpu.VMEM((ns, 1, CH), F32),
                pltpu.VMEM((PARTS, ns, PART, CH), BF16),
                pltpu.VMEM((PARTS, ns, PART, CH), BF16),
                pltpu.VMEM((PARTS, ns, PART, CH), BF16),
                pltpu.VMEM((ns, 32, CH), BF16),
                pltpu.VMEM((1, CH), F32),
                pltpu.VMEM((nh, 1, CH), F32),
                pltpu.VMEM((2, CH), F32),
                pltpu.VMEM((ns, 2, CH), F32),
                pltpu.SemaphoreType.DMA((14,)),
                pltpu.SemaphoreType.DMA((4,)),
                pltpu.SemaphoreType.DMA((2 * (3 + 2 * PARTS),)),
                pltpu.SemaphoreType.DMA((PARTS, ns)),
            ],
            compiler_params=pltpu.CompilerParams(
                collective_id=0, has_side_effects=True, vmem_limit_bytes=40 * 2**20
            ),
        )(*(pltpu.with_memory_space_constraint(array, pltpu.HBM) for array in given))
        return mixed, tgrad.reshape(tokens), kl.reshape(())

    return jax.shard_map(
        per_device,
        mesh=mesh,
        in_specs=(
            P("seq", "head"), P("seq", "head"), P("seq", "head", None, None), P("seq", "head"), P("head"), P("head"),
            P(None, "head"), P(None, "head", None, None), P("head"), P("head"), P("head"), P("seq"), P(), P(),
        ),
        out_specs=(P("seq", "head"), P("seq"), P()),
        check_vma=False,
    )
```

```python
import functools

import jax
import jax.numpy as jnp
from jax import lax
from jax.experimental import pallas as pl
from jax.experimental.pallas import tpu as pltpu
from jax.sharding import PartitionSpec as P

CH = 128
NP = 100
EPS = 1e-05
CAP = 8.0
F32 = jnp.float32
BF16 = jnp.bfloat16
MESH = pl.DeviceIdType.MESH
FAR = (4, 5, 3, 6, 2, 7, 1)
NX, NZ = 4, 8
SHIFTS = sorted(
    ((dx, dz) for dx in range(NX) for dz in range(NZ) if dx or dz),
    key=lambda shift: -min(shift[0], NX - shift[0]) - min(shift[1], NZ - shift[1]),
)
PARTS = 1
PART = 32 // PARTS


def nn(a, b):
    return lax.dot_general(a, b, (((1,), (0,)), ((), ())), preferred_element_type=F32)


def nt(a, b):
    return lax.dot_general(a, b, (((1,), (1,)), ((), ())), preferred_element_type=F32)


def iota(shape, dim):
    return lax.broadcasted_iota(jnp.int32, shape, dim)


def split2(v):
    high = v.astype(BF16)
    return high, (v - high.astype(F32)).astype(BF16)


def split3(v):
    high = v.astype(BF16)
    rest = v - high.astype(F32)
    mid = rest.astype(BF16)
    return high, mid, (rest - mid.astype(F32)).astype(BF16)


def column(row):
    n = row.shape[1]
    return jnp.sum(jnp.where(iota((n, n), 0) == iota((n, n), 1), row, 0.0), axis=1, keepdims=True)


def silu(v):
    below = 1.0 + jnp.exp(-v)
    guess = pl.reciprocal(below, approx=True)
    return v * (guess * (2.0 - below * guess))


def convolve(current, before, taps):
    padded = jnp.concatenate([before, current], axis=0)
    total = jnp.zeros(current.shape, F32)
    for tap in range(4):
        shifted = padded if tap == 3 else pltpu.roll(padded, 3 - tap, 0)
        total = total + shifted[16:] * taps[tap : tap + 1]
    return silu(total).astype(BF16)


def spread_codes(shape, sections):
    row, lane = iota(shape, 0), iota(shape, 1)
    code = jnp.full(shape, -1, jnp.int32)
    for first, last, start, width, size in sections:
        inside = (row >= first) & (row < last) & (lane >= start) & (lane < start + width)
        code = jnp.where(inside, (row & 15) - (lane - start) // size, code)
    return code


def kernel(ns, nh, *refs):
    given, (mixed, tgrad, kl), held = refs[:14], refs[14:17], refs[17:31]
    x, z, bc, dt, bias, alog, convx, convbc, skip, gain, weight, pid, tlogits, torder = held
    (
        xc, cm, bt, mix, paired, tokb, tokc, spreads, codes, local, lg, eg, squares, scored, both, member, prow, tail_x, tail_bc,
        info, info_all, s_send, p1, e_send, p2, h_send, h_all, q_send, q_all,
        in_sem, tail_sem, sems, p2_sem,
    ) = refs[31:]
    me = lax.axis_index("seq")
    mh = lax.axis_index("head")

    def far(i):
        return 4 + (2 * lax.rem(i, 2) - 1) * ((i + 1) // 2)

    def seq_pair(i):
        return lax.rem(me // 4 + far(i), 8)

    def each_seq_peer(act):
        for dx, dz in SHIFTS:
            act(lax.rem(me // NZ + dx, NX) * NZ + lax.rem(lax.rem(me, NZ) + dz, NZ))

    def each_head_peer(act):
        for offset in FAR:
            act(lax.rem(mh + offset, nh))

    barrier = pltpu.get_barrier_semaphore()
    each_seq_peer(lambda peer: pl.semaphore_signal(barrier, inc=1, device_id={"seq": peer}, device_id_type=MESH))
    each_head_peer(lambda peer: pl.semaphore_signal(barrier, inc=1, device_id={"head": peer}, device_id_type=MESH))

    loads = [
        pltpu.make_async_copy(source, target, in_sem.at[i])
        for i, (source, target) in enumerate(zip(given, held))
    ]
    for i in (3, 4, 5, 2, 7, 0, 6, 11, 1, 8, 9, 10, 12, 13):
        loads[i].start()

    codes[...] = spread_codes((CH, 4 * CH), ((0, 32, 0, CH, 64), (32, 64, CH, CH, 64), (64, 112, 2 * CH, 2 * CH, CH)))
    for hp in range(8):
        code = spread_codes((CH, CH), ((0, 32, 0, CH, 64),))
        spreads[:, hp * CH : (hp + 1) * CH] = (code == 2 * hp).astype(F32).astype(BF16)
    squares[...] = jnp.zeros(squares.shape, F32)
    scored[...] = jnp.zeros(scored.shape, F32)

    for i in (3, 4, 5):
        loads[i].wait()
    steps = jax.nn.softplus(dt[...] + column(bias[...]))
    rates = -jnp.exp(column(alog[...])) * steps
    upto = (iota((CH, CH), 0) <= iota((CH, CH), 1)).astype(F32).astype(BF16)
    stacked = jnp.concatenate([rates[:, b * CH : (b + 1) * CH] for b in range(4)], axis=0)
    cumul = sum(nn(part, upto) for part in reversed(split3(stacked)))
    logs = jnp.zeros((16, 1), F32)
    for b in reversed(range(4)):
        here = cumul[16 * b : 16 * b + 16]
        logs = logs + here[:, CH - 1 :]
        parts = split2(jnp.exp(logs - here) * steps[:, b * CH : (b + 1) * CH])
        rows = [part.astype(F32) for part in parts] + [jnp.zeros((96, CH), F32)]
        tokb[b * CH : (b + 1) * CH] = jnp.transpose(jnp.concatenate(rows, axis=0)).astype(BF16)

    even = iota((8, CH), 0) % 2 == 0
    for i in (2, 7):
        loads[i].wait()
    taps = convbc[...].astype(F32)

    def conv_bc(first, count, before):
        current = bc[2 * first : 2 * (first + count)].astype(F32)
        padded = jnp.concatenate([before, current], axis=0)
        total = jnp.zeros((count // 4, 8, CH), F32)
        for tap in range(4):
            shifted = padded if tap == 3 else pltpu.roll(padded, 2 * (3 - tap), 0)
            factor = jnp.where(even, taps[2 * tap : 2 * tap + 1], taps[2 * tap + 1 : 2 * tap + 2])
            total = total + shifted[16:].reshape(count // 4, 8, CH) * factor[None]
        mix[2 * first : 2 * (first + count)] = silu(total).reshape(2 * count, CH)

    def turn_b(b):
        bt[:, b * CH : (b + 1) * CH] = jnp.transpose(mix[pl.ds(2 * b * CH, CH, stride=2)]).astype(BF16)

    for b in range(4):
        conv_bc(b * CH, CH, bc[2 * b * CH - 16 : 2 * b * CH].astype(F32) if b else jnp.zeros((16, CH), F32))
        turn_b(b)
    for i in (0, 6):
        loads[i].wait()

    def local_state(hp):
        lanes = pl.ds(pl.multiple_of(hp * CH, CH), CH)
        factors = convx[:, lanes].astype(F32)
        loaded = []
        for b in range(4):
            at = slice(b * CH, (b + 1) * CH)
            before = x[b * CH - 16 : b * CH, lanes].astype(F32) if b else jnp.zeros((16, CH), F32)
            made = convolve(x[at, lanes].astype(F32), before, factors)
            xc[at, lanes] = made
            part = made.astype(F32) * nn(tokb[at], spreads[:, lanes])
            if b == 0:
                part = jnp.where(iota((CH, CH), 0) >= 3, part, 0.0)
            loaded.append(part.astype(BF16))
        local[:, lanes] = nn(bt[...], jnp.concatenate(loaded, axis=0))

    @pl.loop(0, 4, unroll=2)
    def _(hp):
        local_state(hp)

    pl.semaphore_wait(barrier, ns - 1 + nh - 1)
    tails = [
        pltpu.make_async_remote_copy(
            src_ref=source.at[pl.ds(source.shape[0] - 16, 16)],
            dst_ref=target,
            send_sem=tail_sem.at[2 * i],
            recv_sem=tail_sem.at[2 * i + 1],
            device_id={"seq": lax.rem(me + 1, ns)},
            device_id_type=MESH,
        )
        for i, (source, target) in enumerate(((x, tail_x), (bc, tail_bc)))
    ]
    for copy in tails:
        copy.start()

    @pl.loop(4, 8, unroll=2)
    def _(hp):
        local_state(hp)

    def copy_to(axis, source, target, phase, peer, arrived=None):
        return pltpu.make_async_remote_copy(
            src_ref=source,
            dst_ref=target,
            send_sem=sems.at[2 * phase],
            recv_sem=sems.at[2 * phase + 1] if arrived is None else arrived,
            device_id={axis: peer},
            device_id_type=MESH,
        )

    def wait_all(phase, count, buffer):
        copy_to("seq", buffer.at[pl.ds(0, count)], buffer.at[pl.ds(0, count)], phase, 0).wait_recv()

    def wait_sent(phase, count, buffer):
        copy_to("seq", buffer.at[pl.ds(0, count)], buffer.at[pl.ds(0, count)], phase, 0).wait_send()

    info[...] = jnp.sum(jnp.where(iota((16, CH), 0) == iota((16, CH), 1), logs, 0.0), axis=0, keepdims=True)
    info_all[me] = info[...]
    each_seq_peer(lambda peer: copy_to("seq", info, info_all.at[me], 0, peer).start())

    starts = nn(tokb[0:16], spreads[...])
    for copy in tails:
        copy.wait()
    before_bc = jnp.where(me > 0, tail_bc[...].astype(F32), 0.0)
    conv_bc(0, 16, before_bc)
    first_b = jnp.concatenate([mix[pl.ds(0, 16, stride=2)], jnp.zeros((CH - 16, CH), F32)], axis=0)
    first_b = jnp.transpose(first_b).astype(BF16)[:, :16]
    made = convolve(x[0:16].astype(F32), jnp.where(me > 0, tail_x[...].astype(F32), 0.0), convx[...].astype(F32))
    xc[0:16] = made
    first_x = jnp.where(iota(starts.shape, 0) < 3, made.astype(F32) * starts, 0.0).astype(BF16)
    for hp in range(8):
        lanes = slice(hp * CH, (hp + 1) * CH)
        state = (local[:, lanes] + nn(first_b, first_x[:, lanes])).astype(BF16)
        for a in range(4):
            for q in range(PARTS):
                s_send[q, hp * 4 + a] = state[32 * a + PART * q : 32 * a + PART * (q + 1)]

    def send_states(q):
        each_seq_peer(lambda peer: copy_to("seq", s_send.at[q, peer], p1.at[q, me], 3 + q, peer).start())
        p1[q, me] = s_send[q, me]

    send_states(0)
    for q in range(1, PARTS):
        send_states(q)

    for i in (1, 8, 9, 10, 11, 12, 13):
        loads[i].wait()
    conv_bc(0, CH, before_bc)
    turn_b(0)
    for b in range(4):
        at = slice(b * CH, (b + 1) * CH)
        cm[at] = mix[pl.ds(2 * b * CH + 1, CH, stride=2)].astype(BF16)
        paired[b] = jnp.where(iota((CH, CH), 0) >= iota((CH, CH), 1), nn(cm[at], bt[:, at]), 0.0)
        here = cumul[16 * b : 16 * b + 16]
        parts = split2(jnp.exp(here[:, CH - 1 :] - here) * steps[:, at]) + split2(jnp.exp(here)) + split3(here)
        rows = [part.astype(F32) for part in parts] + [jnp.zeros((16, CH), F32)]
        tokc[at] = jnp.transpose(jnp.concatenate(rows, axis=0)).astype(BF16)
        for h in range(16):
            prow[0, h, :, at] = here[h : h + 1]
    for h in range(16):
        prow[1, h] = steps[h : h + 1]
    skip_column = column(skip[...])

    def inside(hp):
        lanes = pl.ds(pl.multiple_of(hp * CH, CH), CH)
        first = iota((CH, CH), 1) < 64
        spread = (codes[...] == 2 * hp).astype(F32).astype(BF16)
        mine = iota((1, CH), 1) // 64 + 2 * hp == iota((16, 1), 0)
        skips = jnp.sum(jnp.where(mine, skip_column, 0.0), axis=0, keepdims=True)
        state = None
        ahead = jnp.ones((1, CH), F32)
        for b in range(4):
            at = slice(b * CH, (b + 1) * CH)
            wide = nn(tokc[at], spread)
            factor, decay = wide[:, :CH], wide[:, CH : 2 * CH]
            pairs = paired[b]
            values = xc[at, lanes]
            halves = []
            for i in range(2):
                later = wide[:, (i + 2) * CH : (i + 3) * CH]
                earlier = prow[0, 2 * hp + i, :, at]
                step = prow[1, 2 * hp + i, :, at]
                halves.append((pairs * jnp.exp(jnp.minimum(later - earlier, 0.0)) * step).astype(BF16))
            zeros = jnp.zeros_like(values)
            blocks = jnp.concatenate([jnp.where(first, values, zeros), jnp.where(first, zeros, values)], axis=0)
            exact = values.astype(F32)
            total = nn(jnp.concatenate(halves, axis=1), blocks) + skips * exact
            if b:
                total = total + decay * sum(nn(cm[at], part) for part in reversed(split2(state)))
            gate = z[at, lanes].astype(F32)
            gate = gate * (0.5 * jnp.tanh(0.5 * gate) + 0.5)
            lg[at, lanes] = total * gate
            eg[at, lanes] = decay * ahead * gate
            if b < 3:
                added = nn(bt[:, at], (exact * factor).astype(BF16))
                state = decay[CH - 1 :] * state + added if b else added
                ahead = ahead * decay[CH - 1 :]

    @pl.loop(0, 5)
    def _(hp):
        inside(hp)

    lane = iota((1, CH), 1)
    spread = (iota((CH, CH), 0) == 2 * (me // 4) + iota((CH, CH), 1) // 64).astype(F32).astype(BF16)
    wait_all(0, ns - 1, info_all)
    decays = jnp.where(lane < 16, jnp.exp(jnp.sum(info_all[...], axis=1)), 0.0)
    decays = sum(nn(part, spread) for part in reversed(split3(decays)))

    def send_entering(q):
        def act(peer):
            arrived = p2_sem.at[q, me]
            copy_to("seq", e_send.at[q, peer], p2.at[me, pl.ds(PART * q, PART)], 3 + PARTS + q, peer, arrived).start()

        wait_all(3 + q, ns - 1, p1.at[q])
        entering = jnp.zeros((PART, CH), F32)
        for j in range(ns):
            e_send[q, j] = entering.astype(BF16)
            if j < ns - 1:
                entering = decays[j : j + 1] * entering + p1[q, j].astype(F32)
        each_seq_peer(act)
        p2[me, PART * q : PART * (q + 1)] = e_send[q, me]

    for q in range(PARTS):
        send_entering(q)

    @pl.loop(5, 8)
    def _(hp):
        inside(hp)

    member[...] = (iota((CH, 4 * CH), 0) == pid[...]).astype(F32).astype(BF16)
    q_send[1:2] = nt(jnp.ones((8, 4 * CH), BF16), member[...])[0:1]
    valid = lane < NP
    ranks = jnp.where(iota((NP, NP), 0) == torder[...], tlogits[...], 0.0)
    ranks = jnp.sum(ranks, axis=1, keepdims=True)
    teacher = jnp.sum(jnp.where(iota((NP, CH), 0) == iota((NP, CH), 1), ranks, 0.0), axis=0, keepdims=True)
    teacher = teacher - jnp.log(jnp.sum(jnp.where(valid, jnp.exp(teacher), 0.0), axis=1, keepdims=True))
    share = jnp.where(valid, jnp.exp(teacher), 0.0)
    gains = gain[...].astype(F32)
    products = gains * weight[...].astype(F32)
    for hp in range(8):
        both[hp] = products[hp : hp + 1]

    @pl.loop(0, 4, unroll=2)
    def _(step):
        pairs = [seq_pair(2 * step + i) for i in range(2)]
        for hp in pairs:
            for a in range(4):
                peer = 4 * hp + a

                @pl.when(peer != me)
                def _():
                    for q in range(PARTS):
                        piece = p2.at[peer, pl.ds(PART * q, PART)]
                        copy_to("seq", piece, piece, 0, peer, p2_sem.at[q, peer]).wait_recv()

        for b in range(4):
            at = slice(b * CH, (b + 1) * CH)
            power, score = squares[at], scored[at]
            for hp in pairs:
                lanes = pl.ds(pl.multiple_of(hp * CH, CH), CH)
                state = p2[pl.ds(4 * hp, 4)].reshape(CH, CH)
                gated = lg[at, lanes] + eg[at, lanes] * nn(cm[at], state)
                lg[at, lanes] = gated
                power = power + gated * gated
                score = score + gated * both[hp]
            squares[at], scored[at] = power, score

    ones = jnp.ones((16, CH), BF16)
    readout = []
    for b in range(4):
        at = slice(b * CH, (b + 1) * CH)
        power = sum(nt(ones, part) for part in reversed(split3(squares[at])))[0:8]
        plain = sum(nt(ones, part) for part in reversed(split3(scored[at])))[0:8]
        readout.append(plain * lax.rsqrt(power / (8 * CH) + EPS))
    part = sum(nt(part, member[...]) for part in reversed(split3(jnp.concatenate(readout, axis=1))))
    h_send[...] = part[0:1]
    h_all[mh] = part[0:1]
    each_head_peer(lambda peer: copy_to("head", h_send, h_all.at[mh], 1, peer).start())

    for b in range(4):
        at = slice(b * CH, (b + 1) * CH)
        scale = lax.rsqrt(jnp.sum(squares[at], axis=1, keepdims=True) / (8 * CH) + EPS)
        for hp in range(8):
            lanes = slice(hp * CH, (hp + 1) * CH)
            mixed[at, lanes] = (lg[at, lanes] * scale * gains[hp : hp + 1]).astype(BF16)
    wait_all(1, nh - 1, h_all)
    q_send[0:1] = jnp.sum(h_all[...], axis=0)
    q_all[me] = q_send[...]
    each_seq_peer(lambda peer: copy_to("seq", q_send, q_all.at[me], 2, peer).start())
    wait_sent(0, ns - 1, info_all)
    for q in range(PARTS):
        wait_sent(3 + q, ns - 1, s_send.at[q])
        wait_sent(3 + PARTS + q, ns - 1, e_send.at[q])
    wait_sent(1, nh - 1, h_all)
    wait_all(2, ns - 1, q_all)
    totals = jnp.sum(q_all[...], axis=0)
    counts = jnp.where(valid, totals[1:2], 1.0)
    squash = jnp.tanh(totals[0:1] / counts / CAP)
    scores = CAP * squash
    student = scores - jnp.log(jnp.sum(jnp.where(valid, jnp.exp(scores), 0.0), axis=1, keepdims=True))
    kl[...] = jnp.sum(share * (teacher - student), axis=1, keepdims=True)
    coef = (jnp.exp(student) - share) * (1.0 - squash * squash) * (4.0 * CH * ns) / counts
    coef = jnp.broadcast_to(jnp.where(valid, coef, 0.0), (8, CH))
    tgrad[...] = sum(nn(part, member[...]) for part in reversed(split3(coef)))[0:1]
    wait_sent(2, ns - 1, q_all)


def solution(mesh):
    ns, nh = mesh.shape["seq"], mesh.shape["head"]

    def per_device(
        x_in, z_in, bc_in, dt_raw, dt_bias, a_log, conv_x, conv_bc, skip_gain, norm_gain, score_weight, passage_ids,
        teacher_logits, teacher_order,
    ):
        vmem = pl.BlockSpec(memory_space=pltpu.VMEM)
        hbm = pl.BlockSpec(memory_space=pltpu.HBM)
        tokens, width = x_in.shape
        given = (
            x_in,
            z_in,
            bc_in.reshape(2 * tokens, CH),
            dt_raw.T,
            dt_bias[None],
            a_log[None],
            conv_x,
            conv_bc.reshape(8, CH),
            skip_gain[None],
            norm_gain.reshape(8, CH),
            score_weight.reshape(8, CH),
            passage_ids[None],
            teacher_logits[None],
            teacher_order[None],
        )
        mixed, tgrad, kl = pl.pallas_call(
            functools.partial(kernel, ns, nh),
            out_shape=(
                pltpu.VMEM((tokens, width), BF16),
                pltpu.VMEM((1, tokens), F32),
                jax.ShapeDtypeStruct((1, 1), F32),
            ),
            in_specs=[hbm] * 14,
            out_specs=(vmem, vmem, vmem),
            scratch_shapes=[
                *(pltpu.VMEM(array.shape, array.dtype) for array in given),
                pltpu.VMEM((tokens, width), BF16),
                pltpu.VMEM((tokens, CH), BF16),
                pltpu.VMEM((CH, tokens), BF16),
                pltpu.VMEM((2 * tokens, CH), F32),
                pltpu.VMEM((4, CH, CH), F32),
                pltpu.VMEM((tokens, CH), BF16),
                pltpu.VMEM((tokens, CH), BF16),
                pltpu.VMEM((CH, width), BF16),
                pltpu.VMEM((CH, 4 * CH), jnp.int32),
                pltpu.VMEM((CH, width), F32),
                pltpu.VMEM((tokens, width), F32),
                pltpu.VMEM((tokens, width), F32),
                pltpu.VMEM((tokens, CH), F32),
                pltpu.VMEM((tokens, CH), F32),
                pltpu.VMEM((8, 1, CH), F32),
                pltpu.VMEM((CH, tokens), BF16),
                pltpu.VMEM((2, 16, 1, tokens), F32),
                pltpu.VMEM((16, width), BF16),
                pltpu.VMEM((16, CH), BF16),
                pltpu.VMEM((1, CH), F32),
                pltpu.VMEM((ns, 1, CH), F32),
                pltpu.VMEM((PARTS, ns, PART, CH), BF16),
                pltpu.VMEM((PARTS, ns, PART, CH), BF16),
                pltpu.VMEM((PARTS, ns, PART, CH), BF16),
                pltpu.VMEM((ns, 32, CH), BF16),
                pltpu.VMEM((1, CH), F32),
                pltpu.VMEM((nh, 1, CH), F32),
                pltpu.VMEM((2, CH), F32),
                pltpu.VMEM((ns, 2, CH), F32),
                pltpu.SemaphoreType.DMA((14,)),
                pltpu.SemaphoreType.DMA((4,)),
                pltpu.SemaphoreType.DMA((2 * (3 + 2 * PARTS),)),
                pltpu.SemaphoreType.DMA((PARTS, ns)),
            ],
            compiler_params=pltpu.CompilerParams(
                collective_id=0, has_side_effects=True, vmem_limit_bytes=40 * 2**20
            ),
        )(*(pltpu.with_memory_space_constraint(array, pltpu.HBM) for array in given))
        return mixed, tgrad.reshape(tokens), kl.reshape(())

    return jax.shard_map(
        per_device,
        mesh=mesh,
        in_specs=(
            P("seq", "head"), P("seq", "head"), P("seq", "head", None, None), P("seq", "head"), P("head"), P("head"),
            P(None, "head"), P(None, "head", None, None), P("head"), P("head"), P("head"), P("seq"), P(), P(),
        ),
        out_specs=(P("seq", "head"), P("seq"), P()),
        check_vma=False,
    )
```

```python
import functools

import jax
import jax.numpy as jnp
from jax import lax
from jax.experimental import pallas as pl
from jax.experimental.pallas import tpu as pltpu
from jax.sharding import PartitionSpec as P

CH = 128
NP = 100
EPS = 1e-05
CAP = 8.0
F32 = jnp.float32
BF16 = jnp.bfloat16
MESH = pl.DeviceIdType.MESH
FAR = (4, 5, 3, 6, 2, 7, 1)
NX, NZ = 4, 8
SHIFTS = sorted(
    ((dx, dz) for dx in range(NX) for dz in range(NZ) if dx or dz),
    key=lambda shift: -min(shift[0], NX - shift[0]) - min(shift[1], NZ - shift[1]),
)
PARTS = 1
PART = 32 // PARTS


def nn(a, b):
    return lax.dot_general(a, b, (((1,), (0,)), ((), ())), preferred_element_type=F32)


def nt(a, b):
    return lax.dot_general(a, b, (((1,), (1,)), ((), ())), preferred_element_type=F32)


def iota(shape, dim):
    return lax.broadcasted_iota(jnp.int32, shape, dim)


def split2(v):
    high = v.astype(BF16)
    return high, (v - high.astype(F32)).astype(BF16)


def split3(v):
    high = v.astype(BF16)
    rest = v - high.astype(F32)
    mid = rest.astype(BF16)
    return high, mid, (rest - mid.astype(F32)).astype(BF16)


def column(row):
    n = row.shape[1]
    return jnp.sum(jnp.where(iota((n, n), 0) == iota((n, n), 1), row, 0.0), axis=1, keepdims=True)


def silu(v):
    below = 1.0 + jnp.exp(-v)
    guess = pl.reciprocal(below, approx=True)
    return v * (guess * (2.0 - below * guess))


def convolve(current, before, taps):
    padded = jnp.concatenate([before, current], axis=0)
    total = jnp.zeros(current.shape, F32)
    for tap in range(4):
        shifted = padded if tap == 3 else pltpu.roll(padded, 3 - tap, 0)
        total = total + shifted[16:] * taps[tap : tap + 1]
    return silu(total).astype(BF16)


def spread_codes(shape, sections):
    row, lane = iota(shape, 0), iota(shape, 1)
    code = jnp.full(shape, -1, jnp.int32)
    for first, last, start, width, size in sections:
        inside = (row >= first) & (row < last) & (lane >= start) & (lane < start + width)
        code = jnp.where(inside, (row & 15) - (lane - start) // size, code)
    return code


def kernel(ns, nh, *refs):
    given, (mixed, tgrad, kl), held = refs[:14], refs[14:17], refs[17:31]
    x, z, bc, dt, bias, alog, convx, convbc, skip, gain, weight, pid, tlogits, torder = held
    (
        xc, cm, bt, mix, paired, tokb, tokc, spreads, codes, local, lg, eg, squares, scored, both, member, prow, tail_x, tail_bc,
        info, info_all, s_send, p1, e_send, p2, h_send, h_all, q_send, q_all,
        in_sem, tail_sem, sems, p2_sem,
    ) = refs[31:]
    me = lax.axis_index("seq")
    mh = lax.axis_index("head")

    def far(i):
        return 4 + (2 * lax.rem(i, 2) - 1) * ((i + 1) // 2)

    def seq_pair(i):
        return lax.rem(me // 4 + far(i), 8)

    def each_seq_peer(act):
        for dx, dz in SHIFTS:
            act(lax.rem(me // NZ + dx, NX) * NZ + lax.rem(lax.rem(me, NZ) + dz, NZ))

    def each_head_peer(act):
        for offset in FAR:
            act(lax.rem(mh + offset, nh))

    barrier = pltpu.get_barrier_semaphore()
    each_seq_peer(lambda peer: pl.semaphore_signal(barrier, inc=1, device_id={"seq": peer}, device_id_type=MESH))
    each_head_peer(lambda peer: pl.semaphore_signal(barrier, inc=1, device_id={"head": peer}, device_id_type=MESH))

    loads = [
        pltpu.make_async_copy(source, target, in_sem.at[i])
        for i, (source, target) in enumerate(zip(given, held))
    ]
    for i in (3, 4, 5, 2, 7, 0, 6, 11, 1, 8, 9, 10, 12, 13):
        loads[i].start()

    codes[...] = spread_codes((CH, 4 * CH), ((0, 32, 0, CH, 64), (32, 64, CH, CH, 64), (64, 112, 2 * CH, 2 * CH, CH)))
    for hp in range(8):
        code = spread_codes((CH, CH), ((0, 32, 0, CH, 64),))
        spreads[:, hp * CH : (hp + 1) * CH] = (code == 2 * hp).astype(F32).astype(BF16)
    squares[...] = jnp.zeros(squares.shape, F32)
    scored[...] = jnp.zeros(scored.shape, F32)

    for i in (3, 4, 5):
        loads[i].wait()
    steps = jax.nn.softplus(dt[...] + column(bias[...]))
    rates = -jnp.exp(column(alog[...])) * steps
    upto = (iota((CH, CH), 0) <= iota((CH, CH), 1)).astype(F32).astype(BF16)
    stacked = jnp.concatenate([rates[:, b * CH : (b + 1) * CH] for b in range(4)], axis=0)
    cumul = sum(nn(part, upto) for part in reversed(split3(stacked)))
    logs = jnp.zeros((16, 1), F32)
    for b in reversed(range(4)):
        here = cumul[16 * b : 16 * b + 16]
        logs = logs + here[:, CH - 1 :]
        parts = split2(jnp.exp(logs - here) * steps[:, b * CH : (b + 1) * CH])
        rows = [part.astype(F32) for part in parts] + [jnp.zeros((96, CH), F32)]
        tokb[b * CH : (b + 1) * CH] = jnp.transpose(jnp.concatenate(rows, axis=0)).astype(BF16)

    even = iota((8, CH), 0) % 2 == 0
    for i in (2, 7):
        loads[i].wait()
    taps = convbc[...].astype(F32)

    def conv_bc(first, count, before):
        current = bc[2 * first : 2 * (first + count)].astype(F32)
        padded = jnp.concatenate([before, current], axis=0)
        total = jnp.zeros((count // 4, 8, CH), F32)
        for tap in range(4):
            shifted = padded if tap == 3 else pltpu.roll(padded, 2 * (3 - tap), 0)
            factor = jnp.where(even, taps[2 * tap : 2 * tap + 1], taps[2 * tap + 1 : 2 * tap + 2])
            total = total + shifted[16:].reshape(count // 4, 8, CH) * factor[None]
        mix[2 * first : 2 * (first + count)] = silu(total).reshape(2 * count, CH)

    def turn_b(b):
        bt[:, b * CH : (b + 1) * CH] = jnp.transpose(mix[pl.ds(2 * b * CH, CH, stride=2)]).astype(BF16)

    for b in range(4):
        conv_bc(b * CH, CH, bc[2 * b * CH - 16 : 2 * b * CH].astype(F32) if b else jnp.zeros((16, CH), F32))
        turn_b(b)
    for i in (0, 6):
        loads[i].wait()

    def local_state(hp):
        lanes = pl.ds(pl.multiple_of(hp * CH, CH), CH)
        factors = convx[:, lanes].astype(F32)
        loaded = []
        for b in range(4):
            at = slice(b * CH, (b + 1) * CH)
            before = x[b * CH - 16 : b * CH, lanes].astype(F32) if b else jnp.zeros((16, CH), F32)
            made = convolve(x[at, lanes].astype(F32), before, factors)
            xc[at, lanes] = made
            part = made.astype(F32) * nn(tokb[at], spreads[:, lanes])
            if b == 0:
                part = jnp.where(iota((CH, CH), 0) >= 3, part, 0.0)
            loaded.append(part.astype(BF16))
        local[:, lanes] = nn(bt[...], jnp.concatenate(loaded, axis=0))

    @pl.loop(0, 4, unroll=2)
    def _(hp):
        local_state(hp)

    pl.semaphore_wait(barrier, ns - 1 + nh - 1)
    tails = [
        pltpu.make_async_remote_copy(
            src_ref=source.at[pl.ds(source.shape[0] - 16, 16)],
            dst_ref=target,
            send_sem=tail_sem.at[2 * i],
            recv_sem=tail_sem.at[2 * i + 1],
            device_id={"seq": lax.rem(me + 1, ns)},
            device_id_type=MESH,
        )
        for i, (source, target) in enumerate(((x, tail_x), (bc, tail_bc)))
    ]
    for copy in tails:
        copy.start()

    @pl.loop(4, 8, unroll=2)
    def _(hp):
        local_state(hp)

    def copy_to(axis, source, target, phase, peer, arrived=None):
        return pltpu.make_async_remote_copy(
            src_ref=source,
            dst_ref=target,
            send_sem=sems.at[2 * phase],
            recv_sem=sems.at[2 * phase + 1] if arrived is None else arrived,
            device_id={axis: peer},
            device_id_type=MESH,
        )

    def wait_all(phase, count, buffer):
        copy_to("seq", buffer.at[pl.ds(0, count)], buffer.at[pl.ds(0, count)], phase, 0).wait_recv()

    def wait_sent(phase, count, buffer):
        copy_to("seq", buffer.at[pl.ds(0, count)], buffer.at[pl.ds(0, count)], phase, 0).wait_send()

    info[...] = jnp.sum(jnp.where(iota((16, CH), 0) == iota((16, CH), 1), logs, 0.0), axis=0, keepdims=True)
    info_all[me] = info[...]
    each_seq_peer(lambda peer: copy_to("seq", info, info_all.at[me], 0, peer).start())

    starts = nn(tokb[0:16], spreads[...])
    for copy in tails:
        copy.wait()
    before_bc = jnp.where(me > 0, tail_bc[...].astype(F32), 0.0)
    conv_bc(0, 16, before_bc)
    first_b = jnp.concatenate([mix[pl.ds(0, 16, stride=2)], jnp.zeros((CH - 16, CH), F32)], axis=0)
    first_b = jnp.transpose(first_b).astype(BF16)[:, :16]
    made = convolve(x[0:16].astype(F32), jnp.where(me > 0, tail_x[...].astype(F32), 0.0), convx[...].astype(F32))
    xc[0:16] = made
    first_x = jnp.where(iota(starts.shape, 0) < 3, made.astype(F32) * starts, 0.0).astype(BF16)
    for hp in range(8):
        lanes = slice(hp * CH, (hp + 1) * CH)
        state = (local[:, lanes] + nn(first_b, first_x[:, lanes])).astype(BF16)
        for a in range(4):
            for q in range(PARTS):
                s_send[q, hp * 4 + a] = state[32 * a + PART * q : 32 * a + PART * (q + 1)]

    def send_states(q):
        each_seq_peer(lambda peer: copy_to("seq", s_send.at[q, peer], p1.at[q, me], 3 + q, peer).start())
        p1[q, me] = s_send[q, me]

    send_states(0)
    for q in range(1, PARTS):
        send_states(q)

    for i in (1, 8, 9, 10, 11, 12, 13):
        loads[i].wait()
    conv_bc(0, CH, before_bc)
    turn_b(0)
    for b in range(4):
        at = slice(b * CH, (b + 1) * CH)
        cm[at] = mix[pl.ds(2 * b * CH + 1, CH, stride=2)].astype(BF16)
        paired[b] = jnp.where(iota((CH, CH), 0) >= iota((CH, CH), 1), nn(cm[at], bt[:, at]), 0.0)
        here = cumul[16 * b : 16 * b + 16]
        parts = split2(jnp.exp(here[:, CH - 1 :] - here) * steps[:, at]) + split2(jnp.exp(here)) + split3(here)
        rows = [part.astype(F32) for part in parts] + [jnp.zeros((16, CH), F32)]
        tokc[at] = jnp.transpose(jnp.concatenate(rows, axis=0)).astype(BF16)
        for h in range(16):
            prow[0, h, :, at] = here[h : h + 1]
    for h in range(16):
        prow[1, h] = steps[h : h + 1]
    skip_column = column(skip[...])

    def inside(hp):
        lanes = pl.ds(pl.multiple_of(hp * CH, CH), CH)
        first = iota((CH, CH), 1) < 64
        spread = (codes[...] == 2 * hp).astype(F32).astype(BF16)
        mine = iota((1, CH), 1) // 64 + 2 * hp == iota((16, 1), 0)
        skips = jnp.sum(jnp.where(mine, skip_column, 0.0), axis=0, keepdims=True)
        state = None
        ahead = jnp.ones((1, CH), F32)
        for b in range(4):
            at = slice(b * CH, (b + 1) * CH)
            wide = nn(tokc[at], spread)
            factor, decay = wide[:, :CH], wide[:, CH : 2 * CH]
            pairs = paired[b]
            values = xc[at, lanes]
            halves = []
            for i in range(2):
                later = wide[:, (i + 2) * CH : (i + 3) * CH]
                earlier = prow[0, 2 * hp + i, :, at]
                step = prow[1, 2 * hp + i, :, at]
                halves.append((pairs * jnp.exp(jnp.minimum(later - earlier, 0.0)) * step).astype(BF16))
            zeros = jnp.zeros_like(values)
            blocks = jnp.concatenate([jnp.where(first, values, zeros), jnp.where(first, zeros, values)], axis=0)
            exact = values.astype(F32)
            total = nn(jnp.concatenate(halves, axis=1), blocks) + skips * exact
            if b:
                total = total + decay * sum(nn(cm[at], part) for part in reversed(split2(state)))
            gate = z[at, lanes].astype(F32)
            gate = gate * (0.5 * jnp.tanh(0.5 * gate) + 0.5)
            lg[at, lanes] = total * gate
            eg[at, lanes] = decay * ahead * gate
            if b < 3:
                added = nn(bt[:, at], (exact * factor).astype(BF16))
                state = decay[CH - 1 :] * state + added if b else added
                ahead = ahead * decay[CH - 1 :]

    @pl.loop(0, 5)
    def _(hp):
        inside(hp)

    lane = iota((1, CH), 1)
    spread = (iota((CH, CH), 0) == 2 * (me // 4) + iota((CH, CH), 1) // 64).astype(F32).astype(BF16)
    wait_all(0, ns - 1, info_all)
    decays = jnp.where(lane < 16, jnp.exp(jnp.sum(info_all[...], axis=1)), 0.0)
    decays = sum(nn(part, spread) for part in reversed(split3(decays)))

    def send_entering(q):
        def act(peer):
            arrived = p2_sem.at[q, me]
            copy_to("seq", e_send.at[q, peer], p2.at[me, pl.ds(PART * q, PART)], 3 + PARTS + q, peer, arrived).start()

        wait_all(3 + q, ns - 1, p1.at[q])
        entering = jnp.zeros((PART, CH), F32)
        for j in range(ns):
            e_send[q, j] = entering.astype(BF16)
            if j < ns - 1:
                entering = decays[j : j + 1] * entering + p1[q, j].astype(F32)
        each_seq_peer(act)
        p2[me, PART * q : PART * (q + 1)] = e_send[q, me]

    for q in range(PARTS):
        send_entering(q)

    @pl.loop(5, 8)
    def _(hp):
        inside(hp)

    member[...] = (iota((CH, 4 * CH), 0) == pid[...]).astype(F32).astype(BF16)
    q_send[1:2] = nt(jnp.ones((8, 4 * CH), BF16), member[...])[0:1]
    valid = lane < NP
    ranks = jnp.where(iota((NP, NP), 0) == torder[...], tlogits[...], 0.0)
    ranks = jnp.sum(ranks, axis=1, keepdims=True)
    teacher = jnp.sum(jnp.where(iota((NP, CH), 0) == iota((NP, CH), 1), ranks, 0.0), axis=0, keepdims=True)
    teacher = teacher - jnp.log(jnp.sum(jnp.where(valid, jnp.exp(teacher), 0.0), axis=1, keepdims=True))
    share = jnp.where(valid, jnp.exp(teacher), 0.0)
    gains = gain[...].astype(F32)
    products = gains * weight[...].astype(F32)
    for hp in range(8):
        both[hp] = products[hp : hp + 1]

    @pl.loop(0, 4, unroll=2)
    def _(step):
        pairs = [seq_pair(2 * step + i) for i in range(2)]
        for hp in pairs:
            for a in range(4):
                peer = 4 * hp + a

                @pl.when(peer != me)
                def _():
                    for q in range(PARTS):
                        piece = p2.at[peer, pl.ds(PART * q, PART)]
                        copy_to("seq", piece, piece, 0, peer, p2_sem.at[q, peer]).wait_recv()

        for b in range(4):
            at = slice(b * CH, (b + 1) * CH)
            power, score = squares[at], scored[at]
            for hp in pairs:
                lanes = pl.ds(pl.multiple_of(hp * CH, CH), CH)
                state = p2[pl.ds(4 * hp, 4)].reshape(CH, CH)
                gated = lg[at, lanes] + eg[at, lanes] * nn(cm[at], state)
                lg[at, lanes] = gated
                power = power + gated * gated
                score = score + gated * both[hp]
            squares[at], scored[at] = power, score

    ones = jnp.ones((16, CH), BF16)
    readout = []
    for b in range(4):
        at = slice(b * CH, (b + 1) * CH)
        power = sum(nt(ones, part) for part in reversed(split3(squares[at])))[0:8]
        plain = sum(nt(ones, part) for part in reversed(split3(scored[at])))[0:8]
        readout.append(plain * lax.rsqrt(power / (8 * CH) + EPS))
    part = sum(nt(part, member[...]) for part in reversed(split3(jnp.concatenate(readout, axis=1))))
    h_send[...] = part[0:1]
    h_all[mh] = part[0:1]
    each_head_peer(lambda peer: copy_to("head", h_send, h_all.at[mh], 1, peer).start())

    for b in range(4):
        at = slice(b * CH, (b + 1) * CH)
        scale = lax.rsqrt(jnp.sum(squares[at], axis=1, keepdims=True) / (8 * CH) + EPS)
        for hp in range(8):
            lanes = slice(hp * CH, (hp + 1) * CH)
            mixed[at, lanes] = (lg[at, lanes] * scale * gains[hp : hp + 1]).astype(BF16)
    wait_all(1, nh - 1, h_all)
    q_send[0:1] = jnp.sum(h_all[...], axis=0)
    q_all[me] = q_send[...]
    each_seq_peer(lambda peer: copy_to("seq", q_send, q_all.at[me], 2, peer).start())
    wait_sent(0, ns - 1, info_all)
    for q in range(PARTS):
        wait_sent(3 + q, ns - 1, s_send.at[q])
        wait_sent(3 + PARTS + q, ns - 1, e_send.at[q])
    wait_sent(1, nh - 1, h_all)
    wait_all(2, ns - 1, q_all)
    totals = jnp.sum(q_all[...], axis=0)
    counts = jnp.where(valid, totals[1:2], 1.0)
    squash = jnp.tanh(totals[0:1] / counts / CAP)
    scores = CAP * squash
    student = scores - jnp.log(jnp.sum(jnp.where(valid, jnp.exp(scores), 0.0), axis=1, keepdims=True))
    kl[...] = jnp.sum(share * (teacher - student), axis=1, keepdims=True)
    coef = (jnp.exp(student) - share) * (1.0 - squash * squash) * (4.0 * CH * ns) / counts
    coef = jnp.broadcast_to(jnp.where(valid, coef, 0.0), (8, CH))
    tgrad[...] = sum(nn(part, member[...]) for part in reversed(split3(coef)))[0:1]
    wait_sent(2, ns - 1, q_all)


def solution(mesh):
    ns, nh = mesh.shape["seq"], mesh.shape["head"]

    def per_device(
        x_in, z_in, bc_in, dt_raw, dt_bias, a_log, conv_x, conv_bc, skip_gain, norm_gain, score_weight, passage_ids,
        teacher_logits, teacher_order,
    ):
        vmem = pl.BlockSpec(memory_space=pltpu.VMEM)
        hbm = pl.BlockSpec(memory_space=pltpu.HBM)
        tokens, width = x_in.shape
        given = (
            x_in,
            z_in,
            bc_in.reshape(2 * tokens, CH),
            dt_raw.T,
            dt_bias[None],
            a_log[None],
            conv_x,
            conv_bc.reshape(8, CH),
            skip_gain[None],
            norm_gain.reshape(8, CH),
            score_weight.reshape(8, CH),
            passage_ids[None],
            teacher_logits[None],
            teacher_order[None],
        )
        mixed, tgrad, kl = pl.pallas_call(
            functools.partial(kernel, ns, nh),
            out_shape=(
                pltpu.VMEM((tokens, width), BF16),
                pltpu.VMEM((1, tokens), F32),
                jax.ShapeDtypeStruct((1, 1), F32),
            ),
            in_specs=[hbm] * 14,
            out_specs=(vmem, vmem, vmem),
            scratch_shapes=[
                *(pltpu.VMEM(array.shape, array.dtype) for array in given),
                pltpu.VMEM((tokens, width), BF16),
                pltpu.VMEM((tokens, CH), BF16),
                pltpu.VMEM((CH, tokens), BF16),
                pltpu.VMEM((2 * tokens + 8, CH), F32),
                pltpu.VMEM((4, CH, CH), F32),
                pltpu.VMEM((tokens, CH), BF16),
                pltpu.VMEM((tokens, CH), BF16),
                pltpu.VMEM((CH, width), BF16),
                pltpu.VMEM((CH, 4 * CH), jnp.int32),
                pltpu.VMEM((CH, width), F32),
                pltpu.VMEM((tokens, width), F32),
                pltpu.VMEM((tokens, width), F32),
                pltpu.VMEM((tokens, CH), F32),
                pltpu.VMEM((tokens, CH), F32),
                pltpu.VMEM((8, 1, CH), F32),
                pltpu.VMEM((CH, tokens), BF16),
                pltpu.VMEM((2, 16, 1, tokens), F32),
                pltpu.VMEM((16, width), BF16),
                pltpu.VMEM((16, CH), BF16),
                pltpu.VMEM((1, CH), F32),
                pltpu.VMEM((ns, 1, CH), F32),
                pltpu.VMEM((PARTS, ns, PART, CH), BF16),
                pltpu.VMEM((PARTS, ns, PART, CH), BF16),
                pltpu.VMEM((PARTS, ns, PART, CH), BF16),
                pltpu.VMEM((ns, 32, CH), BF16),
                pltpu.VMEM((1, CH), F32),
                pltpu.VMEM((nh, 1, CH), F32),
                pltpu.VMEM((2, CH), F32),
                pltpu.VMEM((ns, 2, CH), F32),
                pltpu.SemaphoreType.DMA((14,)),
                pltpu.SemaphoreType.DMA((4,)),
                pltpu.SemaphoreType.DMA((2 * (3 + 2 * PARTS),)),
                pltpu.SemaphoreType.DMA((PARTS, ns)),
            ],
            compiler_params=pltpu.CompilerParams(
                collective_id=0, has_side_effects=True, vmem_limit_bytes=40 * 2**20
            ),
        )(*(pltpu.with_memory_space_constraint(array, pltpu.HBM) for array in given))
        return mixed, tgrad.reshape(tokens), kl.reshape(())

    return jax.shard_map(
        per_device,
        mesh=mesh,
        in_specs=(
            P("seq", "head"), P("seq", "head"), P("seq", "head", None, None), P("seq", "head"), P("head"), P("head"),
            P(None, "head"), P(None, "head", None, None), P("head"), P("head"), P("head"), P("seq"), P(), P(),
        ),
        out_specs=(P("seq", "head"), P("seq"), P()),
        check_vma=False,
    )
```
